128 devices in a mesh: dp: 32 (over z, y, core), sp: 4 (over x).
Axes of the slice: x: 4, y: 4, z: 4, core: 2. Of those that a mesh axis runs over, the one named last changes fastest.
Arguments:
- tokens: bfloat16 [32768, 8192], P(('dp', 'sp')), may hold values from -24 to 24
- value_projection_matrix: bfloat16 [8192, 512], P(('dp', 'sp')), may hold values from -0.0625 to 0.0625
- queries: bfloat16 [32768, 4096], P(('dp', 'sp')), may hold values from -80 to 80, as said below
- rotated_key_rows: bfloat16 [32768, 512], P(('dp', 'sp')), may hold values from -80 to 80, as said below
- output_cotangent: bfloat16 [32768, 4096], P(('dp', 'sp')), may hold values from -6 to 6
- block_dest: int32 [4096], P(('dp', 'sp')), may hold values from 0 to 4095, as said below
- doc_ids: int32 [32, 1024], P('dp'), may hold values from 0 to 1, as said below
Outputs:
- query_gradient: bfloat16 [32768, 4096], P(('dp', 'sp'))
- key_gradient: bfloat16 [32768, 512], P(('dp', 'sp'))
- weight_grad: float32 [8192, 512], P(('dp', 'sp'))
The draws below stay inside these ranges and needn't reach their ends.
Inputs may be any that keep to these rules, and one draw needn't show every extreme that they name: block_dest is a permutation of the 4096 blocks; block b belongs to device b // 32 and lands in group-order block block_dest[b], held by device block_dest[b] // 32, which lies in the same sp index; every device receives exactly 32 blocks; at most 2 blocks pass from one device to one device; along dp, block k of a device of sp index j moves a number of places (cyclically) that depends only on j and k. `doc_ids`: in each group the ids start at 0 and never fall; equal ids form one document; a group holds one or two documents, and a second one begins between positions 256 and 768. `queries`: rows g * 1024 to (g + 1) * 1024 - 1 are the positions of group g in order. `rotated_key_rows`: rows g * 1024 to (g + 1) * 1024 - 1 are the positions of group g in order.
All inputs are finite; a program needn't handle non-finite values.
Results may differ from the reference program's by a relative error of at most 0.02.
Values may be sent and summed in bfloat16 or wider, within the bound.
A program may use at most 128 MiB of HBM per device.

```python
import math
import jax
import jax.numpy as jnp
from jax import lax

MODEL_WIDTH = 8192
HEAD_SIZE = 128
QUERY_HEADS = 32
KEY_VALUE_HEADS = 4
TOK_DEV = 256
BLK = 8
GROUP_POSITIONS = 1024
TOKEN_TOTAL = 32768
N_DP = 32
N_SP = 4


def document_ids(key):
    key = jax.random.fold_in(key, 101)
    count_key, fill_key, cut_key = jax.random.split(key, 3)
    two_docs = jax.random.randint(count_key, (N_DP,), 0, 2)
    fullest = jax.random.randint(fill_key, (), 0, N_DP)
    two_docs = two_docs.at[fullest].set(1)
    cuts = jax.random.randint(cut_key, (N_DP,), GROUP_POSITIONS // 4, 3 * GROUP_POSITIONS // 4 + 1)
    positions = jnp.arange(GROUP_POSITIONS, dtype=jnp.int32)
    second = (two_docs[:, None] == 1) & (positions[None, :] >= cuts[:, None])
    return second.astype(jnp.int32)


def draw_doc_ids(key, part):
    return document_ids(key)


def draw_rotated_key_rows(key, part):
    key = jax.random.fold_in(key, 303)
    return jax.random.normal(key, (TOKEN_TOTAL, KEY_VALUE_HEADS * HEAD_SIZE), jnp.float32).astype(jnp.bfloat16)


def draw_queries(key, part):
    key = jax.random.fold_in(key, 404)
    return jax.random.normal(key, (TOKEN_TOTAL, QUERY_HEADS * HEAD_SIZE), jnp.float32).astype(jnp.bfloat16)


def draw_block_dest(key, part):
    key = jax.random.fold_in(key, 9)
    block_count = TOK_DEV // BLK
    order_key, label_key, rotation_key = jax.random.split(key, 3)
    baseline = jnp.arange(block_count, dtype=jnp.int32) % N_DP
    baseline = baseline.at[1].set(0)
    ordering = jax.vmap(lambda lane_key: jax.random.permutation(lane_key, block_count))(jax.random.split(order_key, N_SP))
    relabel = jax.vmap(lambda lane_key: jax.random.permutation(lane_key, N_DP))(jax.random.split(label_key, N_SP))
    offsets = jnp.take_along_axis(relabel, baseline[ordering], axis=1)
    rotation = jax.random.randint(rotation_key, (N_DP * N_SP,), 0, block_count)
    blocks_all = jnp.arange(TOKEN_TOTAL // BLK, dtype=jnp.int32)
    source = blocks_all // block_count
    local_block = blocks_all % block_count
    sp_lane = source % N_SP
    dp_row = source // N_SP
    dest_device = (dp_row + offsets[sp_lane, local_block]) % N_DP * N_SP + sp_lane
    target = (local_block + rotation[dest_device]) % block_count
    return (dest_device * block_count + target).astype(jnp.int32)


def strengthened(values, key, source, target, blocks, factor):
    owner, partner = [(jnp.arange(values.shape[axis_at]) // (values.shape[axis_at] // blocks)).reshape([-1 if axis == axis_at else 1 for axis in range(values.ndim)]) for axis_at in (source, target)]
    chosen = jax.random.permutation(key, blocks)[partner]
    strong = (owner == chosen) | (owner == (partner + blocks // 2) % blocks)
    return jnp.where(strong, factor * values, values)


def block_levels(rng, dims, cuts, least, high):
    loudness, own = 1.0, jax.random.fold_in(rng, 6)
    for axis_at, blocks in cuts:
        steps = jnp.exp(jax.random.uniform(jax.random.fold_in(own, axis_at), (blocks,), jnp.float32, least / len(cuts), high / len(cuts)))
        loudness = loudness * jnp.repeat(steps, dims[axis_at] // blocks).reshape([-1 if axis == axis_at else 1 for axis in range(len(dims))])
    return loudness


def bell_draw(rng, dims, scale, bound, pieces=(), kind=jnp.bfloat16):
    values = scale * jax.random.normal(rng, dims, jnp.float32)
    if pieces:
        values = values * block_levels(rng, dims, pieces, -0.22, 0.18)
    return jnp.clip(values, -bound, bound).astype(kind)


def noise_with(stream_key, extent, spread, most, cuts, heavy, kind=jnp.bfloat16):
    drawn = spread * jax.random.normal(stream_key, extent, jnp.float32)
    if cuts:
        drawn = drawn * block_levels(stream_key, extent, cuts, -0.22, 0.18)
    return jnp.clip(strengthened(drawn, jax.random.fold_in(stream_key, 3), *heavy), -most, most).astype(kind)


def setup_inputs(seed: int = 0) -> dict:
    seeds = jax.random.split(jax.random.key(seed), 8)
    tokens = noise_with(seeds[0], (TOKEN_TOTAL, MODEL_WIDTH), 1.0, 24.0, ((0, 128),), (0, 1, 128, 5.5))
    value_projection_matrix = bell_draw(seeds[1], (MODEL_WIDTH, KEY_VALUE_HEADS * HEAD_SIZE), MODEL_WIDTH ** -0.5, 0.0625, ((0, 128),))
    queries = draw_queries(jax.random.fold_in(seeds[7], 71), 0)
    rotated_key_rows = draw_rotated_key_rows(jax.random.fold_in(seeds[7], 71), 0)
    output_cotangent = bell_draw(seeds[4], (TOKEN_TOTAL, QUERY_HEADS * HEAD_SIZE), 1.0, 6.0, ((0, 128),))
    block_dest = draw_block_dest(jax.random.fold_in(seeds[7], 71), 0)
    doc_ids = draw_doc_ids(jax.random.fold_in(seeds[7], 71), 0)
    return {"tokens": tokens, "value_projection_matrix": value_projection_matrix, "queries": queries, "rotated_key_rows": rotated_key_rows, "output_cotangent": output_cotangent, "block_dest": block_dest, "doc_ids": doc_ids}


def attend_group(group_args):
    queries, rotated_key_rows, projected_values, output_cotangent, doc = group_args
    heads_per_group = QUERY_HEADS // KEY_VALUE_HEADS
    score_scale = 1.0 / math.sqrt(HEAD_SIZE)
    query_function = queries.astype(jnp.float32).reshape(GROUP_POSITIONS, KEY_VALUE_HEADS, heads_per_group, HEAD_SIZE)
    key_function = rotated_key_rows.astype(jnp.float32).reshape(GROUP_POSITIONS, KEY_VALUE_HEADS, HEAD_SIZE)
    value_function = projected_values.astype(jnp.float32).reshape(GROUP_POSITIONS, KEY_VALUE_HEADS, HEAD_SIZE)
    gradient_function = output_cotangent.astype(jnp.float32).reshape(GROUP_POSITIONS, KEY_VALUE_HEADS, heads_per_group, HEAD_SIZE)
    positions = jnp.arange(GROUP_POSITIONS, dtype=jnp.int32)
    allowed = (doc[:, None] == doc[None, :]) & (positions[None, :] <= positions[:, None])
    scores = jnp.einsum('qgrd,kgd->grqk', query_function, key_function) * score_scale
    scores = jnp.where(allowed, scores, -1e+30)
    row_max = lax.optimization_barrier(jnp.max(scores, axis=-1, keepdims=True))
    weights_raw = jnp.exp(scores - row_max)
    probability = weights_raw / lax.optimization_barrier(jnp.sum(weights_raw, axis=-1, keepdims=True))
    prob_low = lax.optimization_barrier(probability.astype(jnp.bfloat16)).astype(jnp.float32)
    attended = jnp.einsum('grqk,kgd->qgrd', prob_low, value_function)
    row_dot = lax.optimization_barrier(jnp.sum(gradient_function * attended, axis=-1))
    dprob = jnp.einsum('qgrd,kgd->grqk', gradient_function, value_function)
    dscore = probability * (dprob - jnp.transpose(row_dot, (1, 2, 0))[..., None])
    dscore_low = lax.optimization_barrier(dscore.astype(jnp.bfloat16)).astype(jnp.float32)
    query_gradient = (jnp.einsum('grqk,kgd->qgrd', dscore_low, key_function) * score_scale).astype(jnp.bfloat16)
    key_gradient = (jnp.einsum('grqk,qgrd->kgd', dscore_low, query_function) * score_scale).astype(jnp.bfloat16)
    value_gradient = jnp.einsum('grqk,qgrd->kgd', prob_low, gradient_function).astype(jnp.bfloat16)
    return (query_gradient.reshape(GROUP_POSITIONS, QUERY_HEADS * HEAD_SIZE), key_gradient.reshape(GROUP_POSITIONS, KEY_VALUE_HEADS * HEAD_SIZE), value_gradient.reshape(GROUP_POSITIONS, KEY_VALUE_HEADS * HEAD_SIZE))

def reference(tokens, value_projection_matrix, queries, rotated_key_rows, output_cotangent, block_dest, doc_ids):
    value_feature_width = KEY_VALUE_HEADS * HEAD_SIZE
    projected_values = jnp.dot(tokens, value_projection_matrix, preferred_element_type=jnp.float32).astype(jnp.bfloat16)
    blocks = projected_values.reshape(TOKEN_TOTAL // BLK, BLK, value_feature_width)
    placed = jnp.zeros_like(blocks).at[block_dest].set(blocks).reshape(N_DP, GROUP_POSITIONS, value_feature_width)
    query_gradient, key_gradient, value_gradient = lax.map(attend_group, (queries.reshape(N_DP, GROUP_POSITIONS, QUERY_HEADS * HEAD_SIZE), rotated_key_rows.reshape(N_DP, GROUP_POSITIONS, value_feature_width), placed, output_cotangent.reshape(N_DP, GROUP_POSITIONS, QUERY_HEADS * HEAD_SIZE), doc_ids))
    grad_blocks = value_gradient.reshape(TOKEN_TOTAL // BLK, BLK, value_feature_width)
    loader_grad = grad_blocks[block_dest].reshape(TOKEN_TOTAL, value_feature_width)
    weight_grad = lax.dot_general(tokens, loader_grad, (((0,), (0,)), ((), ())), preferred_element_type=jnp.float32)
    return (query_gradient.reshape(TOKEN_TOTAL, QUERY_HEADS * HEAD_SIZE), key_gradient.reshape(TOKEN_TOTAL, value_feature_width), weight_grad)
```

```python
import functools
import math

import jax
import jax.numpy as jnp
from jax import lax
from jax.experimental import pallas as pl
from jax.experimental.pallas import tpu as pltpu
from jax.sharding import PartitionSpec as P

MESH = pl.DeviceIdType.MESH
BF = jnp.bfloat16
F32 = jnp.float32
HEADS = 32
KV_HEADS = 4
HEAD = 128
ROWS = 256
KEYS = 1024
FEAT = 512
SLOTS = 512
BLK = 8
SCALE = 1.0 / math.sqrt(HEAD)
LOG2E = math.log2(math.e)


def nn(a, b):
    return lax.dot_general(a, b, (((1,), (0,)), ((), ())), preferred_element_type=F32)


def nt(a, b):
    return lax.dot_general(a, b, (((1,), (1,)), ((), ())), preferred_element_type=F32)


def tn(a, b):
    return lax.dot_general(a, b, (((0,), (0,)), ((), ())), preferred_element_type=F32)


def kernel(
    tok_hbm, w_hbm, q_hbm, k_hbm, do_hbm, pos_ref, lab_ref, doc_ref,
    dq_hbm, dk_ref, wg_ref,
    tok, wh, qv, dov, dqv, kf, kt, vf, prob, inv_row, bias, acc, part, part_in,
    snd, rcv, lsnd, lrcv, fwd, bwd_t, bsnd, brcv, dvl,
    gsend, gin, f1a, f2a, f1b, f2b, mpa, mma, mpb, mmb, s2a, s2b, s3,
    loc_sem, tl_sem, ts_sem, tr_sem, wx_s, wx_r, w2_s, w2_r, w3_s, w3_r, k_s, k_r,
    l_s, l_r, a_s, a_r, b_s, b_r, p_s, p_r, d_s, d_r, v_s, v_r, dv_s, dv_r, dk_s, dk_r,
    g_s, g_r, g2_s, g2_r, g3_s, g3_r, dq_s,
):
    me = lax.axis_index("dp")
    x = lax.axis_index("sp")
    z, y, c = me // 8, (me // 2) % 4, me % 2

    def at(zz, yy, xx):
        return (zz * 8 + yy * 2 + c, xx)

    def up(v, o):
        return (v + o) % 4

    def along_x(o):
        return at(z, y, up(x, o))

    def along_y(o):
        return at(z, up(y, o), x)

    def along_z(o):
        return at(up(z, o), y, x)

    sibling = (z * 8 + y * 2 + (1 - c), x)

    def remote(src, dst, ss, rs, dev):
        return pltpu.make_async_remote_copy(src, dst, ss, rs, device_id=dev, device_id_type=MESH)

    own_w = pltpu.make_async_copy(w_hbm, wh.at[z, y, pl.ds(x * 64, 64)], loc_sem.at[0])
    own_k = pltpu.make_async_copy(k_hbm, kf.at[pl.ds(x * ROWS, ROWS)], loc_sem.at[1])
    own_q = pltpu.make_async_copy(q_hbm, qv, loc_sem.at[2])
    own_do = pltpu.make_async_copy(do_hbm, dov, loc_sem.at[3])
    own_w.start()
    own_k.start()
    own_q.start()
    own_do.start()

    def tok_local(i):
        return pltpu.make_async_copy(
            tok_hbm.at[:, pl.ds((i * 2 + c) * 256, 256)],
            tok.at[pl.ds(0, ROWS), pl.ds(i * 256, 256)], tl_sem.at[i])

    def tok_remote(i):
        return remote(
            tok_hbm.at[:, pl.ds((i * 2 + 1 - c) * 256, 256)],
            tok.at[pl.ds(ROWS, ROWS), pl.ds(i * 256, 256)], ts_sem.at[i], tr_sem.at[i], sibling)

    barrier = pltpu.get_barrier_semaphore()

    def greet(o, carry):
        pl.semaphore_signal(barrier, inc=1, device_id=((me + o) % 32, x), device_id_type=MESH)
        return carry

    lax.fori_loop(1, 32, greet, 0)
    for o in (1, 2, 3):
        pl.semaphore_signal(barrier, inc=1, device_id=along_x(o), device_id_type=MESH)
    pl.semaphore_wait(barrier, 34)

    def w_x(o):
        return remote(w_hbm, wh.at[z, y, pl.ds(x * 64, 64)], wx_s.at[o], wx_r.at[o], along_x(o))

    def k_x(o, e):
        i = (o - 1) * 4 + e
        cols = pl.ds(e * HEAD, HEAD)
        return remote(k_hbm.at[:, cols], kf.at[pl.ds(x * ROWS, ROWS), cols], k_s.at[i], k_r.at[i], along_x(o))

    for o in (1, 3, 2):
        w_x(o).start()
    for e in range(KV_HEADS):
        for o in (1, 3, 2):
            k_x(o, e).start()

    r_i = lax.broadcasted_iota(jnp.int32, (SLOTS, ROWS), 0)
    c_i = lax.broadcasted_iota(jnp.int32, (SLOTS, ROWS), 1)
    same_row = (r_i % BLK) == (c_i % BLK)
    fwd[...] = jnp.where(same_row & ((r_i // BLK) == pos_ref[0:1, :]), 1.0, 0.0).astype(BF)
    lsnd[...] = nn(fwd[...], lab_ref[...]).astype(BF)

    def peers(send_buf, recv_buf, ss, rs):
        def one(o):
            p = (me + o) % 32
            return remote(send_buf.at[pl.ds(p * 16, 16)], recv_buf.at[pl.ds(me * 16, 16)], ss.at[o], rs.at[o], (p, x))

        def start():
            def body(o, carry):
                one(o).start()
                return carry

            lax.fori_loop(1, 32, body, 0)
            mine = pl.ds(pl.multiple_of(me * 16, 16), 16)
            recv_buf[mine, :] = send_buf[mine, :]

        def wait_recv():
            def body(o, carry):
                one(o).wait_recv()
                return carry

            lax.fori_loop(1, 32, body, 0)

        def wait_send():
            def body(o, carry):
                one(o).wait_send()
                return carry

            lax.fori_loop(1, 32, body, 0)

        return start, wait_recv, wait_send

    l_start, l_recv, l_done = peers(lsnd, lrcv, l_s, l_r)
    a_start, a_recv, a_done = peers(snd, rcv, a_s, a_r)
    b_start, b_recv, b_done = peers(bsnd, brcv, b_s, b_r)
    l_start()

    def start_tokens(i, carry):
        tok_local(i).start()
        tok_remote(i).start()
        return carry

    lax.fori_loop(0, 16, start_tokens, 0)

    cut = jnp.sum(jnp.where(doc_ref[0:1, :] == 0, 1, 0), axis=1, keepdims=True)
    k_pos = lax.broadcasted_iota(jnp.int32, (KEYS, ROWS), 0)
    q_pos = lax.broadcasted_iota(jnp.int32, (KEYS, ROWS), 1) + x * ROWS
    allowed = (k_pos <= q_pos) & ((k_pos < cut) == (q_pos < cut))
    bias[...] = jnp.where(allowed, 0.0, -1e30)

    def w_2a(o):
        blk = wh.at[z, y, pl.ds(0, 128)]
        return remote(blk, blk, w2_s.at[o], w2_r.at[o], along_y(o))

    def w_2b(o):
        blk = wh.at[z, y, pl.ds(128, 128)]
        return remote(blk, blk, w2_s.at[4 + o], w2_r.at[4 + o], along_z(o))

    def w_3a(j, m):
        yy = up(y, j)
        if m < 2:
            blk = wh.at[z, yy, pl.ds(0, 128)]
        elif m == 2:
            blk = wh.at[up(z, 3), yy, pl.ds(0, 64)]
        else:
            blk = wh.at[up(z, 1), yy, pl.ds(64, 64)]
        i = j * 4 + m
        return remote(blk, blk, w3_s.at[i], w3_r.at[i], along_z(1 if m % 2 == 0 else 3))

    def w_3b(j, m):
        zz = up(z, j)
        if m < 2:
            blk = wh.at[zz, y, pl.ds(128, 128)]
        elif m == 2:
            blk = wh.at[zz, up(y, 3), pl.ds(128, 64)]
        else:
            blk = wh.at[zz, up(y, 1), pl.ds(192, 64)]
        i = 16 + j * 4 + m
        return remote(blk, blk, w3_s.at[i], w3_r.at[i], along_y(1 if m % 2 == 0 else 3))

    def w_begin():
        own_w.wait()
        for o in (1, 3, 2):
            w_x(o).wait_recv()
        for o in (1, 3, 2):
            w_2a(o).start()
            w_2b(o).start()
        for m in (0, 1):
            w_3a(0, m).start()
            w_3b(0, m).start()

    def w_full(j):
        w_2a((4 - j) % 4).wait_recv()
        w_2b((4 - j) % 4).wait_recv()
        for m in (0, 1):
            w_3a(j, m).start()
            w_3b(j, m).start()

    def w_forward(j):
        for m in (0, 1):
            w_3a(j, m).wait_recv()
            w_3a(j, m + 2).start()
            w_3b(j, m).wait_recv()
            w_3b(j, m + 2).start()

    def w_end():
        for j in (0, 1, 3, 2):
            for m in (2, 3):
                w_3a(j, m).wait_recv()
                w_3b(j, m).wait_recv()
        for o in (1, 2, 3):
            w_x(o).wait_send()
            w_2a(o).wait_send()
            w_2b(o).wait_send()
        for j in range(4):
            for m in range(4):
                w_3a(j, m).wait_send()
                w_3b(j, m).wait_send()

    def sum_x(ss, rs):
        def one(o, e):
            i = (o - 1) * 4 + e
            cols = pl.ds(e * HEAD, HEAD)
            return remote(gsend.at[pl.ds(up(x, o) * ROWS, ROWS), cols], gin.at[o - 1, :, cols], ss.at[i], rs.at[i], along_x(o))

        def start(e):
            cols = pl.ds(e * HEAD, HEAD)
            gsend[:, cols] = acc[:, cols].astype(BF)
            for o in (1, 3, 2):
                one(o, e).start()

        def finish():
            for e in range(KV_HEADS):
                for o in (1, 3, 2):
                    one(o, e).wait_recv()
            own = acc[pl.ds(pl.multiple_of(x * ROWS, ROWS), ROWS), :]
            total = own + gin[0].astype(F32) + gin[1].astype(F32) + gin[2].astype(F32)
            for e in range(KV_HEADS):
                for o in (1, 3, 2):
                    one(o, e).wait_send()
            return total

        return start, finish

    dv_start, dv_finish = sum_x(dv_s, dv_r)
    dk_start, dk_finish = sum_x(dk_s, dk_r)

    def at_head(h, where, act):
        pl.when(h == where)(act)

    w_begin()
    own_q.wait()
    own_do.wait()
    own_k.wait()

    def first(h, carry):
        e = h // 8
        for i in range(KV_HEADS):
            @pl.when(h == 8 * i)
            def _():
                for o in (1, 3, 2):
                    k_x(o, i).wait_recv()
        at_head(h, 3, lambda: w_full(1))
        at_head(h, 5, lambda: w_full(3))
        at_head(h, 7, lambda: w_full(2))
        at_head(h, 11, lambda: w_forward(0))
        at_head(h, 16, lambda: w_forward(1))
        at_head(h, 22, lambda: w_forward(3))
        at_head(h, 28, lambda: w_forward(2))
        ecol = pl.ds(pl.multiple_of(e * HEAD, HEAD), HEAD)
        hcol = pl.ds(pl.multiple_of(h * HEAD, HEAD), HEAD)
        s = nt(kf[:, ecol], qv[:, hcol]) * (SCALE * LOG2E) + bias[...]
        m = jnp.max(s, axis=0, keepdims=True)
        p = jnp.exp2(s - m)
        inv = 1.0 / jnp.sum(p, axis=0, keepdims=True)
        low = p.astype(BF)
        prob[h] = low
        inv_row[h] = inv
        inv_rows = jnp.transpose(jnp.broadcast_to(inv, (HEAD, ROWS)))
        do = (dov[:, hcol].astype(F32) * inv_rows).astype(BF)
        dov[:, hcol] = do
        add = nn(low, do)

        @pl.when(h % 8 == 0)
        def _():
            acc[:, ecol] = add

        @pl.when(h % 8 != 0)
        def _():
            acc[:, ecol] += add

        for i in range(KV_HEADS):
            at_head(h, 8 * i + 7, lambda i=i: dv_start(i))
        return carry

    lax.fori_loop(0, HEADS, first, 0)

    l_recv()
    lab = lrcv[...].astype(F32)
    want = (c_i // BLK + 1).astype(F32)
    bwd_t[...] = jnp.where(same_row & (jnp.concatenate([lab, lab], axis=1) == want), 1.0, 0.0).astype(BF)
    bsnd[...] = nn(bwd_t[...], dv_finish().astype(BF)).astype(BF)
    b_start()

    def tokens_in(i, carry):
        tok_local(i).wait()
        tok_remote(i).wait_recv()
        return carry

    lax.fori_loop(0, 16, tokens_in, 0)
    w_end()

    def project(first_row):
        total = None
        for zz in range(4):
            term = nn(tok[pl.ds(first_row, ROWS), pl.ds(zz * 1024, 1024)], wh[zz].reshape(1024, FEAT))
            total = term if total is None else total + term
        return total

    give_part = remote(part, part_in, p_s.at[0], p_r.at[0], sibling)
    part[...] = project(ROWS)
    give_part.start()
    mine = project(0)
    give_part.wait_recv()
    values = (mine + part_in[...]).astype(BF)
    snd[...] = nn(fwd[...], values).astype(BF)
    a_start()

    b_recv()
    dvl[pl.ds(0, ROWS), :] = tn(fwd[...], brcv[...]).astype(BF)
    give_dvl = remote(dvl.at[pl.ds(0, ROWS)], dvl.at[pl.ds(ROWS, ROWS)], d_s.at[0], d_r.at[0], sibling)
    give_dvl.start()
    give_dvl.wait_recv()

    def weight_block(i, carry):
        cols = pl.ds(pl.multiple_of(i * 256, 256), 256)
        wh[i // 4, i % 4] = tn(tok[:, cols], dvl[...]).astype(BF)
        return carry

    lax.fori_loop(0, 16, weight_block, 0)

    a_rows, b_rows = pl.ds(0, 128), pl.ds(128, 128)
    low2, high2 = pl.ds(0, 2), pl.ds(2, 2)

    g_1 = [
        remote(wh.at[up(z, 2), low2, a_rows], f1a, g_s.at[0], g_r.at[0], along_z(1)),
        remote(wh.at[up(z, 2), high2, a_rows], f2a, g_s.at[1], g_r.at[1], along_z(3)),
        remote(wh.at[low2, up(y, 2), b_rows], f1b, g_s.at[2], g_r.at[2], along_y(1)),
        remote(wh.at[high2, up(y, 2), b_rows], f2b, g_s.at[3], g_r.at[3], along_y(3)),
        remote(wh.at[up(z, 1), high2, a_rows], mpa.at[high2], g_s.at[4], g_r.at[4], along_z(1)),
        remote(wh.at[up(z, 3), low2, a_rows], mma.at[low2], g_s.at[5], g_r.at[5], along_z(3)),
        remote(wh.at[high2, up(y, 1), b_rows], mpb.at[high2], g_s.at[6], g_r.at[6], along_y(1)),
        remote(wh.at[low2, up(y, 3), b_rows], mmb.at[low2], g_s.at[7], g_r.at[7], along_y(3)),
    ]
    g_2 = [
        remote(wh.at[up(z, 1), low2, a_rows], mpa.at[low2], g_s.at[8], g_r.at[8], along_z(1)),
        remote(wh.at[up(z, 3), high2, a_rows], mma.at[high2], g_s.at[9], g_r.at[9], along_z(3)),
        remote(wh.at[low2, up(y, 1), b_rows], mpb.at[low2], g_s.at[10], g_r.at[10], along_y(1)),
        remote(wh.at[high2, up(y, 3), b_rows], mmb.at[high2], g_s.at[11], g_r.at[11], along_y(3)),
    ]

    def g_3a(o):
        return remote(wh.at[z, up(y, o), a_rows], s2a.at[o - 1], g2_s.at[o], g2_r.at[o], along_y(o))

    def g_3b(o):
        return remote(wh.at[up(z, o), y, b_rows], s2b.at[o - 1], g2_s.at[4 + o], g2_r.at[4 + o], along_z(o))

    def g_x(o):
        rows = pl.ds(up(x, o) * 64, 64)
        return remote(wh.at[z, y, rows], s3.at[o - 1], g3_s.at[o], g3_r.at[o], along_x(o))

    def bsum(*terms):
        total = terms[0].astype(F32)
        for t in terms[1:]:
            total = total + t.astype(F32)
        return total

    def g_step1():
        for i in range(4):
            g_1[i].wait_recv()
            if i == 0:
                wh[up(z, 1), 0:2, 0:128] = bsum(wh[up(z, 1), 0:2, 0:128], f1a[...]).astype(BF)
            elif i == 1:
                wh[up(z, 3), 2:4, 0:128] = bsum(wh[up(z, 3), 2:4, 0:128], f2a[...]).astype(BF)
            elif i == 2:
                wh[0:2, up(y, 1), 128:256] = bsum(wh[0:2, up(y, 1), 128:256], f1b[...]).astype(BF)
            else:
                wh[2:4, up(y, 3), 128:256] = bsum(wh[2:4, up(y, 3), 128:256], f2b[...]).astype(BF)
            g_2[i].start()

    def g_step2():
        for i in range(4, 8):
            g_1[i].wait_recv()
        for d in g_2:
            d.wait_recv()
        for i in range(4):
            wh[z, i, 0:128] = bsum(wh[z, i, 0:128], mpa[i], mma[i]).astype(BF)
            wh[i, y, 128:256] = bsum(wh[i, y, 128:256], mpb[i], mmb[i]).astype(BF)
        for o in (1, 3, 2):
            g_3a(o).start()
            g_3b(o).start()

    def g_step3():
        for o in (1, 3, 2):
            g_3a(o).wait_recv()
            g_3b(o).wait_recv()
        wh[z, y, 0:128] = bsum(wh[z, y, 0:128], s2a[0], s2a[1], s2a[2]).astype(BF)
        wh[z, y, 128:256] = bsum(wh[z, y, 128:256], s2b[0], s2b[1], s2b[2]).astype(BF)
        for o in (1, 3, 2):
            g_x(o).start()

    def g_step4():
        for o in (1, 3, 2):
            g_x(o).wait_recv()
        rows = pl.ds(pl.multiple_of(x * 64, 64), 64)
        wg_ref[...] = bsum(wh[z, y, rows, :], s3[0], s3[1], s3[2])
        for d in g_1 + g_2:
            d.wait_send()
        for o in (1, 2, 3):
            g_3a(o).wait_send()
            g_3b(o).wait_send()
            g_x(o).wait_send()

    for d in g_1:
        d.start()

    a_recv()
    mine_rows = pl.ds(pl.multiple_of(x * ROWS, ROWS), ROWS)
    vf[mine_rows, :] = tn(bwd_t[...], rcv[...]).astype(BF)

    def v_x(o, e):
        i = (o - 1) * 4 + e
        blk = vf.at[pl.ds(x * ROWS, ROWS), pl.ds(e * HEAD, HEAD)]
        return remote(blk, blk, v_s.at[i], v_r.at[i], along_x(o))

    for e in range(KV_HEADS):
        for o in (1, 3, 2):
            v_x(o, e).start()
    for e in range(KV_HEADS):
        kt[e] = jnp.transpose(kf[:, pl.ds(e * HEAD, HEAD)].astype(F32)).astype(BF)

    def dq_out(e):
        cols = pl.ds(e * 1024, 1024)
        return pltpu.make_async_copy(dqv.at[:, cols], dq_hbm.at[:, cols], dq_s.at[e])

    def second(h, carry):
        e = h // 8
        for i in range(KV_HEADS):
            @pl.when(h == 8 * i)
            def _():
                for o in (1, 3, 2):
                    v_x(o, i).wait_recv()
        at_head(h, 2, g_step1)
        at_head(h, 20, g_step2)
        at_head(h, 29, g_step3)
        ecol = pl.ds(pl.multiple_of(e * HEAD, HEAD), HEAD)
        hcol = pl.ds(pl.multiple_of(h * HEAD, HEAD), HEAD)
        do = dov[:, hcol]
        dp = nt(vf[:, ecol], do)
        p = prob[h].astype(F32)
        rd = jnp.sum(p * dp, axis=0, keepdims=True) * inv_row[h]
        ds = (p * (dp - rd)).astype(BF)
        add = nn(ds, qv[:, hcol])

        @pl.when(h % 8 == 0)
        def _():
            acc[:, ecol] = add

        @pl.when(h % 8 != 0)
        def _():
            acc[:, ecol] += add

        dq_t = nn(kt[e], ds) * SCALE
        dqv[:, hcol] = jnp.transpose(dq_t).astype(BF)
        for i in range(KV_HEADS):
            @pl.when(h == 8 * i + 7)
            def _():
                dk_start(i)
                dq_out(i).start()
        return carry

    lax.fori_loop(0, HEADS, second, 0)

    dk_ref[...] = (dk_finish() * SCALE).astype(BF)
    g_step4()

    for e in range(KV_HEADS):
        dq_out(e).wait()
        for o in (1, 2, 3):
            k_x(o, e).wait_send()
            v_x(o, e).wait_send()
    l_done()
    a_done()
    b_done()
    give_part.wait_send()
    give_dvl.wait_send()

    def tokens_out(i, carry):
        tok_remote(i).wait_send()
        return carry

    lax.fori_loop(0, 16, tokens_out, 0)


def per_device(tokens, w, queries, keys, cotangent, block_dest, doc_ids):
    dest_dp = block_dest // 128
    target = block_dest % 32
    earlier = jnp.arange(32)[None, :] < jnp.arange(32)[:, None]
    rank = jnp.sum(((dest_dp[None, :] == dest_dp[:, None]) & earlier).astype(jnp.int32), axis=1)
    pos = jnp.broadcast_to(jnp.repeat(dest_dp * 2 + rank, BLK)[None, :], (8, ROWS))
    lab = jnp.broadcast_to(jnp.repeat(target + 1, BLK)[:, None], (ROWS, 128)).astype(BF)
    doc = jnp.broadcast_to(doc_ids, (8, KEYS))
    vm = lambda shape, t: pltpu.VMEM(shape, t)
    dma = lambda n: pltpu.SemaphoreType.DMA((n,))
    anyspec = pl.BlockSpec(memory_space=pl.ANY)
    vspec = pl.BlockSpec(memory_space=pltpu.VMEM)
    scratch = [
        vm((512, 4096), BF),
        vm((4, 4, 256, FEAT), BF),
        vm((ROWS, 4096), BF),
        vm((ROWS, 4096), BF),
        vm((ROWS, 4096), BF),
        vm((KEYS, FEAT), BF),
        vm((KV_HEADS, HEAD, KEYS), BF),
        vm((KEYS, FEAT), BF),
        vm((HEADS, KEYS, ROWS), BF),
        vm((HEADS, 1, ROWS), F32),
        vm((KEYS, ROWS), F32),
        vm((KEYS, FEAT), F32),
        vm((ROWS, FEAT), F32),
        vm((ROWS, FEAT), F32),
        vm((SLOTS, FEAT), BF),
        vm((SLOTS, FEAT), BF),
        vm((SLOTS, 128), BF),
        vm((SLOTS, 128), BF),
        vm((SLOTS, ROWS), BF),
        vm((SLOTS, ROWS), BF),
        vm((SLOTS, FEAT), BF),
        vm((SLOTS, FEAT), BF),
        vm((512, FEAT), BF),
        vm((KEYS, FEAT), BF),
        vm((3, ROWS, FEAT), BF),
        vm((2, 128, FEAT), BF),
        vm((2, 128, FEAT), BF),
        vm((2, 128, FEAT), BF),
        vm((2, 128, FEAT), BF),
        vm((4, 128, FEAT), BF),
        vm((4, 128, FEAT), BF),
        vm((4, 128, FEAT), BF),
        vm((4, 128, FEAT), BF),
        vm((3, 128, FEAT), BF),
        vm((3, 128, FEAT), BF),
        vm((3, 64, FEAT), BF),
        dma(4), dma(16), dma(16), dma(16),
        dma(4), dma(4), dma(8), dma(8), dma(32), dma(32), dma(12), dma(12),
        dma(32), dma(32), dma(32), dma(32), dma(32), dma(32),
        dma(1), dma(1), dma(1), dma(1),
        dma(12), dma(12), dma(12), dma(12), dma(12), dma(12),
        dma(12), dma(12), dma(8), dma(8), dma(4), dma(4), dma(4),
    ]
    return pl.pallas_call(
        kernel,
        out_shape=(
            jax.ShapeDtypeStruct((ROWS, 4096), BF),
            jax.ShapeDtypeStruct((ROWS, FEAT), BF),
            jax.ShapeDtypeStruct((64, FEAT), F32),
        ),
        in_specs=[anyspec] * 5 + [vspec] * 3,
        out_specs=(anyspec, vspec, vspec),
        scratch_shapes=scratch,
        compiler_params=pltpu.CompilerParams(
            collective_id=0, has_side_effects=True, vmem_limit_bytes=62 * 1024 * 1024
        ),
        name="attention_and_weights",
    )(tokens, w, queries, keys, cotangent, pos, lab, doc)


def solution(mesh):
    both = P(("dp", "sp"), None)
    return jax.shard_map(
        per_device,
        mesh=mesh,
        in_specs=(both, both, both, both, both, P(("dp", "sp")), P("dp", None)),
        out_specs=(both, both, both),
        check_vma=False,
    )
```

```python
import functools
import math

import jax
import jax.numpy as jnp
from jax import lax
from jax.experimental import pallas as pl
from jax.experimental.pallas import tpu as pltpu
from jax.sharding import PartitionSpec as P

MESH = pl.DeviceIdType.MESH
BF = jnp.bfloat16
F32 = jnp.float32
HEADS = 32
KV_HEADS = 4
HEAD = 128
ROWS = 256
KEYS = 1024
FEAT = 512
SLOTS = 512
BLK = 8
SCALE = 1.0 / math.sqrt(HEAD)
LOG2E = math.log2(math.e)


def nn(a, b):
    return lax.dot_general(a, b, (((1,), (0,)), ((), ())), preferred_element_type=F32)


def nt(a, b):
    return lax.dot_general(a, b, (((1,), (1,)), ((), ())), preferred_element_type=F32)


def tn(a, b):
    return lax.dot_general(a, b, (((0,), (0,)), ((), ())), preferred_element_type=F32)


def kernel(
    tok_hbm, w_hbm, q_hbm, k_hbm, do_hbm, dest_ref, doc_ref,
    dq_hbm, dk_ref, wg_ref,
    tok, wh, qs, dos, kf, kt, vf, prob, inv_row, bias, acc, part, part_in,
    snd, rcv, lsnd, lrcv, fwd, bwd_t, bsnd, brcv, dvl,
    gsend, gin, f1a, f2a, f1b, f2b, mpa, mma, mpb, mmb, s2a, s2b, s3,
    loc_sem, q_sem, do_sem, tl_sem, ts_sem, tr_sem, wx_s, wx_r, w2_s, w2_r, w3_s, w3_r, k_s, k_r,
    l_s, l_r, a_s, a_r, b_s, b_r, p_s, p_r, d_s, d_r, v_s, v_r, dv_s, dv_r, dk_s, dk_r,
    g_s, g_r, g2_s, g2_r, g3_s, g3_r, dq_s, relay,
):
    me = lax.axis_index("dp")
    x = lax.axis_index("sp")
    z, y, c = me // 8, (me // 2) % 4, me % 2

    def at(zz, yy, xx):
        return (zz * 8 + yy * 2 + c, xx)

    def up(v, o):
        return (v + o) % 4

    def along_x(o):
        return at(z, y, up(x, o))

    def along_y(o):
        return at(z, up(y, o), x)

    def along_z(o):
        return at(up(z, o), y, x)

    sibling = (z * 8 + y * 2 + (1 - c), x)

    def remote(src, dst, ss, rs, dev):
        return pltpu.make_async_remote_copy(src, dst, ss, rs, device_id=dev, device_id_type=MESH)

    def landed(ref, sem):
        pltpu.make_async_copy(ref, ref, sem).wait()

    own_w = pltpu.make_async_copy(w_hbm, wh.at[z, y, pl.ds(x * 64, 64)], loc_sem.at[0])
    own_k = pltpu.make_async_copy(k_hbm, kf.at[pl.ds(x * ROWS, ROWS)], loc_sem.at[1])

    def head_in(src, dst, sem, h):
        return pltpu.make_async_copy(
            src.at[:, pl.ds(h * HEAD, HEAD)], dst.at[h // 8, pl.ds((h % 8) * ROWS, ROWS)], sem.at[h // 8])

    def q_in(h):
        return head_in(q_hbm, qs, q_sem, h)

    def do_in(h):
        return head_in(do_hbm, dos, do_sem, h)

    def tok_local(i):
        return pltpu.make_async_copy(
            tok_hbm.at[:, pl.ds((i * 2 + c) * 256, 256)],
            tok.at[pl.ds(0, ROWS), pl.ds(i * 256, 256)], tl_sem.at[0])

    def tok_remote(i):
        return remote(
            tok_hbm.at[:, pl.ds((i * 2 + 1 - c) * 256, 256)],
            tok.at[pl.ds(ROWS, ROWS), pl.ds(i * 256, 256)], ts_sem.at[0], tr_sem.at[0], sibling)

    barrier = pltpu.get_barrier_semaphore()

    for o in (1, 2, 3):
        across = (up(z, o) * 8 + y * 2 + (1 - c), x)
        for partner in (along_x(o), along_y(o), along_z(o), across):
            pl.semaphore_signal(barrier, inc=1, device_id=partner, device_id_type=MESH)
    pl.semaphore_signal(barrier, inc=1, device_id=sibling, device_id_type=MESH)
    own_k.start()
    own_w.start()

    def heads_in(h, carry):
        q_in(h).start()
        do_in(h).start()
        return carry

    lax.fori_loop(0, HEADS, heads_in, 0)

    cut = jnp.sum(jnp.where(doc_ref[0:1, :] == 0, 1, 0), axis=1, keepdims=True)
    k_pos = lax.broadcasted_iota(jnp.int32, (KEYS, ROWS), 0)
    q_pos = lax.broadcasted_iota(jnp.int32, (KEYS, ROWS), 1) + x * ROWS
    allowed = (k_pos <= q_pos) & ((k_pos < cut) == (q_pos < cut))
    bias[...] = jnp.where(allowed, 0.0, -1e30)

    blk = lax.broadcasted_iota(jnp.int32, (8, ROWS), 1) // BLK
    dest = jnp.zeros((8, ROWS), jnp.int32)
    for b in range(32):
        dest = jnp.where(blk == b, dest_ref[b], dest)
    dest_dp, target = dest // 128, dest % 32
    rank = jnp.zeros((8, ROWS), jnp.int32)
    for b in range(31):
        rank = rank + jnp.where((blk > b) & (dest_dp == dest_ref[b] // 128), 1, 0)
    pos = (dest_dp * 2 + rank)[0:1, :]
    r_i = lax.broadcasted_iota(jnp.int32, (SLOTS, ROWS), 0)
    c_i = lax.broadcasted_iota(jnp.int32, (SLOTS, ROWS), 1)
    same_row = (r_i % BLK) == (c_i % BLK)
    fwd[...] = jnp.where(same_row & ((r_i // BLK) == pos), 1.0, 0.0).astype(BF)
    lab_rows = jnp.broadcast_to((target + 1).astype(F32)[0:1, :], (HEAD, ROWS))
    lsnd[...] = nn(fwd[...], jnp.transpose(lab_rows).astype(BF)).astype(BF)
    pl.semaphore_wait(barrier, 13)
    for o in (1, 2, 3):
        pl.semaphore_signal(relay, inc=1, device_id=along_y(o), device_id_type=MESH)

    def w_x(o):
        return remote(w_hbm, wh.at[z, y, pl.ds(x * 64, 64)], wx_s.at[0], wx_r.at[0], along_x(o))

    def k_x(o, e):
        cols = pl.ds(e * HEAD, HEAD)
        return remote(k_hbm.at[:, cols], kf.at[pl.ds(x * ROWS, ROWS), cols], k_s.at[0], k_r.at[e], along_x(o))

    for o in (1, 3, 2):
        k_x(o, 0).start()
        w_x(o).start()

    def peers(send_buf, recv_buf, ss, rs):
        def one(o):
            p = (me + o) % 32
            return remote(send_buf.at[pl.ds(p * 16, 16)], recv_buf.at[pl.ds(me * 16, 16)], ss.at[0], rs.at[0], (p, x))

        def start():
            def body(o, carry):
                one(o).start()
                return carry

            lax.fori_loop(1, 32, body, 0)
            mine = pl.ds(pl.multiple_of(me * 16, 16), 16)
            recv_buf[mine, :] = send_buf[mine, :]

        def wait_recv():
            landed(recv_buf.at[pl.ds(0, 496)], rs.at[0])

        def wait_send():
            landed(send_buf.at[pl.ds(0, 496)], ss.at[0])

        return start, wait_recv, wait_send

    l_start, l_recv, l_done = peers(lsnd, lrcv, l_s, l_r)
    a_start, a_recv, a_done = peers(snd, rcv, a_s, a_r)
    b_start, b_recv, b_done = peers(bsnd, brcv, b_s, b_r)

    def start_tokens(i, carry):
        tok_local(i).start()
        tok_remote(i).start()
        return carry


    def w_2a(o):
        blk = wh.at[z, y, pl.ds(0, 128)]
        return remote(blk, blk, w2_s.at[0], w2_r.at[o], along_y(o))

    def w_2b(o):
        blk = wh.at[z, y, pl.ds(128, 128)]
        return remote(blk, blk, w2_s.at[0], w2_r.at[4 + o], along_z(o))

    def w_3a(j, m):
        yy = up(y, j)
        if m < 2:
            blk = wh.at[z, yy, pl.ds(0, 128)]
        elif m == 2:
            blk = wh.at[up(z, 3), yy, pl.ds(0, 64)]
        else:
            blk = wh.at[up(z, 1), yy, pl.ds(64, 64)]
        i = j * 2 + m if m < 2 else 16
        return remote(blk, blk, w3_s.at[0], w3_r.at[i], along_z(1 if m % 2 == 0 else 3))

    def w_3b(j, m):
        zz = up(z, j)
        if m < 2:
            blk = wh.at[zz, y, pl.ds(128, 128)]
        elif m == 2:
            blk = wh.at[zz, up(y, 3), pl.ds(128, 64)]
        else:
            blk = wh.at[zz, up(y, 1), pl.ds(192, 64)]
        i = 8 + j * 2 + m if m < 2 else 16
        return remote(blk, blk, w3_s.at[0], w3_r.at[i], along_y(1 if m % 2 == 0 else 3))

    def w_begin():
        own_w.wait()
        landed(wh.at[0, 0, pl.ds(0, 192)], wx_r.at[0])
        for o in (1, 3, 2):
            w_2a(o).start()
            w_2b(o).start()
        for m in (0, 1):
            w_3a(0, m).start()
            w_3b(0, m).start()

    def w_full(j):
        w_2a((4 - j) % 4).wait_recv()
        w_2b((4 - j) % 4).wait_recv()
        for m in (0, 1):
            w_3a(j, m).start()
            w_3b(j, m).start()

    def w_forward(j):
        for m in (0, 1):
            w_3a(j, m).wait_recv()
            w_3a(j, m + 2).start()
            w_3b(j, m).wait_recv()
            w_3b(j, m + 2).start()

    def w_end():
        landed(wh.at[0], w3_r.at[16])
        landed(wh.at[0, 0, pl.ds(0, 192)], wx_s.at[0])
        landed(wh.at[0, pl.ds(0, 3)], w2_s.at[0])
        landed(wh.at[pl.ds(0, 3)], w3_s.at[0])

    def sum_x(ss, rs):
        def one(o, e):
            cols = pl.ds(e * HEAD, HEAD)
            return remote(gsend.at[pl.ds(up(x, o) * ROWS, ROWS), cols], gin.at[o - 1, :, cols], ss.at[0], rs.at[0], along_x(o))

        def start(e):
            cols = pl.ds(e * HEAD, HEAD)
            gsend[:, cols] = acc[:, cols].astype(BF)
            for o in (1, 3, 2):
                one(o, e).start()

        def finish():
            landed(gin, rs.at[0])
            own = acc[pl.ds(pl.multiple_of(x * ROWS, ROWS), ROWS), :]
            total = own + gin[0].astype(F32) + gin[1].astype(F32) + gin[2].astype(F32)
            landed(gin, ss.at[0])
            return total

        return start, finish

    dv_start, dv_finish = sum_x(dv_s, dv_r)
    dk_start, dk_finish = sum_x(dk_s, dk_r)

    def at_head(h, where, act):
        pl.when(h == where)(act)

    own_k.wait()

    def three(e):
        return kf.at[pl.ds(0, 768), pl.ds(e * HEAD, HEAD)]

    def k_send(e):
        for o in (1, 3, 2):
            k_x(o, e).start()

    def w_rest():
        for j in (1, 3, 2):
            w_full(j)
        w_forward(0)

    w_begin()
    k_send(1)
    k_send(2)
    pl.semaphore_wait(relay, 3)
    l_start()
    lax.fori_loop(0, 16, start_tokens, 0)

    def first(e, carry):
        for i in range(KV_HEADS):
            @pl.when(e == i)
            def _():
                landed(three(i), k_r.at[i])
                if i == 1:
                    k_send(3)
        at_head(e, 2, w_rest)
        at_head(e, 3, lambda: w_forward(1))
        landed(qs.at[e], q_sem.at[e])
        landed(dos.at[e], do_sem.at[e])
        ecol = pl.ds(pl.multiple_of(e * HEAD, HEAD), HEAD)
        keys = kf[:, ecol]
        for hh in range(8):
            rows = slice(hh * ROWS, (hh + 1) * ROWS)
            s = nt(keys, qs[e, rows, :]) * (SCALE * LOG2E) + bias[...]
            m = jnp.max(s, axis=0, keepdims=True)
            p = jnp.exp2(s - m)
            inv = 1.0 / jnp.sum(p, axis=0, keepdims=True)
            prob[e, :, rows] = p.astype(BF)
            inv_row[e * 8 + hh] = inv
            inv_rows = jnp.transpose(jnp.broadcast_to(inv, (HEAD, ROWS)))
            dos[e, rows, :] = (dos[e, rows, :].astype(F32) * inv_rows).astype(BF)
        acc[:, ecol] = nn(prob[e], dos[e])
        for i in range(KV_HEADS):
            at_head(e, i, lambda i=i: dv_start(i))
        return carry

    lax.fori_loop(0, KV_HEADS, first, 0)
    w_forward(3)
    l_recv()
    lab = lrcv[...].astype(F32)
    want = (c_i // BLK + 1).astype(F32)
    bwd_t[...] = jnp.where(same_row & (jnp.concatenate([lab, lab], axis=1) == want), 1.0, 0.0).astype(BF)
    w_forward(2)

    bsnd[...] = nn(bwd_t[...], dv_finish().astype(BF)).astype(BF)
    b_start()

    landed(tok.at[pl.ds(0, ROWS)], tl_sem.at[0])
    landed(tok.at[pl.ds(ROWS, ROWS)], tr_sem.at[0])
    w_end()

    def project(first_row):
        total = None
        for zz in range(4):
            term = nn(tok[pl.ds(first_row, ROWS), pl.ds(zz * 1024, 1024)], wh[zz].reshape(1024, FEAT))
            total = term if total is None else total + term
        return total

    give_part = remote(part, part_in, p_s.at[0], p_r.at[0], sibling)
    part[...] = project(ROWS)
    give_part.start()
    mine = project(0)
    give_part.wait_recv()
    values = (mine + part_in[...]).astype(BF)
    snd[...] = nn(fwd[...], values).astype(BF)
    a_start()

    b_recv()
    dvl[pl.ds(0, ROWS), :] = tn(fwd[...], brcv[...]).astype(BF)
    give_dvl = remote(dvl.at[pl.ds(0, ROWS)], dvl.at[pl.ds(ROWS, ROWS)], d_s.at[0], d_r.at[0], sibling)
    give_dvl.start()
    give_dvl.wait_recv()

    def weight_blocks(i, carry):
        for n in range(8):
            cols = pl.ds(pl.multiple_of(i * 2048 + n * 256, 256), 256)
            wh[i * 2 + n // 4, n % 4] = tn(tok[:, cols], dvl[...]).astype(BF)
        return carry

    lax.fori_loop(0, 2, weight_blocks, 0)

    a_rows, b_rows = pl.ds(0, 128), pl.ds(128, 128)
    low2, high2 = pl.ds(0, 2), pl.ds(2, 2)

    g_1 = [
        remote(wh.at[up(z, 2), low2, a_rows], f1a, g_s.at[0], g_r.at[0], along_z(1)),
        remote(wh.at[up(z, 2), high2, a_rows], f2a, g_s.at[0], g_r.at[1], along_z(3)),
        remote(wh.at[low2, up(y, 2), b_rows], f1b, g_s.at[0], g_r.at[2], along_y(1)),
        remote(wh.at[high2, up(y, 2), b_rows], f2b, g_s.at[0], g_r.at[3], along_y(3)),
        remote(wh.at[up(z, 1), high2, a_rows], mpa.at[high2], g_s.at[0], g_r.at[4], along_z(1)),
        remote(wh.at[up(z, 3), low2, a_rows], mma.at[low2], g_s.at[0], g_r.at[5], along_z(3)),
        remote(wh.at[high2, up(y, 1), b_rows], mpb.at[high2], g_s.at[0], g_r.at[6], along_y(1)),
        remote(wh.at[low2, up(y, 3), b_rows], mmb.at[low2], g_s.at[0], g_r.at[7], along_y(3)),
    ]
    g_2 = [
        remote(wh.at[up(z, 1), low2, a_rows], mpa.at[low2], g_s.at[0], g_r.at[4], along_z(1)),
        remote(wh.at[up(z, 3), high2, a_rows], mma.at[high2], g_s.at[0], g_r.at[5], along_z(3)),
        remote(wh.at[low2, up(y, 1), b_rows], mpb.at[low2], g_s.at[0], g_r.at[6], along_y(1)),
        remote(wh.at[high2, up(y, 3), b_rows], mmb.at[high2], g_s.at[0], g_r.at[7], along_y(3)),
    ]

    def g_3a(o):
        return remote(wh.at[z, up(y, o), a_rows], s2a.at[o - 1], g2_s.at[0], g2_r.at[0], along_y(o))

    def g_3b(o):
        return remote(wh.at[up(z, o), y, b_rows], s2b.at[o - 1], g2_s.at[0], g2_r.at[1], along_z(o))

    def g_x(o):
        rows = pl.ds(up(x, o) * 64, 64)
        return remote(wh.at[z, y, rows], s3.at[o - 1], g3_s.at[0], g3_r.at[0], along_x(o))

    def bsum(*terms):
        total = terms[0].astype(F32)
        for t in terms[1:]:
            total = total + t.astype(F32)
        return total

    def g_step1():
        for i in range(4):
            g_1[i].wait_recv()
            if i == 0:
                wh[up(z, 1), 0:2, 0:128] = bsum(wh[up(z, 1), 0:2, 0:128], f1a[...]).astype(BF)
            elif i == 1:
                wh[up(z, 3), 2:4, 0:128] = bsum(wh[up(z, 3), 2:4, 0:128], f2a[...]).astype(BF)
            elif i == 2:
                wh[0:2, up(y, 1), 128:256] = bsum(wh[0:2, up(y, 1), 128:256], f1b[...]).astype(BF)
            else:
                wh[2:4, up(y, 3), 128:256] = bsum(wh[2:4, up(y, 3), 128:256], f2b[...]).astype(BF)
            g_2[i].start()

    def g_step2():
        for i, buf in enumerate((mpa, mma, mpb, mmb)):
            landed(buf, g_r.at[4 + i])
        for i in range(4):
            wh[z, i, 0:128] = bsum(wh[z, i, 0:128], mpa[i], mma[i]).astype(BF)
            wh[i, y, 128:256] = bsum(wh[i, y, 128:256], mpb[i], mmb[i]).astype(BF)
        for o in (1, 3, 2):
            g_3a(o).start()
            g_3b(o).start()

    def g_step3():
        landed(s2a, g2_r.at[0])
        landed(s2b, g2_r.at[1])
        wh[z, y, 0:128] = bsum(wh[z, y, 0:128], s2a[0], s2a[1], s2a[2]).astype(BF)
        wh[z, y, 128:256] = bsum(wh[z, y, 128:256], s2b[0], s2b[1], s2b[2]).astype(BF)
        for o in (1, 3, 2):
            g_x(o).start()

    def g_step4():
        landed(s3, g3_r.at[0])
        rows = pl.ds(pl.multiple_of(x * 64, 64), 64)
        wg_ref[...] = bsum(wh[z, y, rows, :], s3[0], s3[1], s3[2])
        landed(wh.at[pl.ds(0, 3)], g_s.at[0])
        landed(wh.at[0, pl.ds(0, 3)], g2_s.at[0])
        landed(s3, g3_s.at[0])

    for d in g_1[:4]:
        d.start()

    a_recv()
    mine_rows = pl.ds(pl.multiple_of(x * ROWS, ROWS), ROWS)
    vf[mine_rows, :] = tn(bwd_t[...], rcv[...]).astype(BF)

    def v_x(o, e):
        blk = vf.at[pl.ds(x * ROWS, ROWS), pl.ds(e * HEAD, HEAD)]
        return remote(blk, blk, v_s.at[0], v_r.at[e], along_x(o))

    def v_send(e):
        for o in (1, 3, 2):
            v_x(o, e).start()

    v_send(0)
    for d in g_1[4:]:
        d.start()
    v_send(1)
    g_step1()
    for e in range(KV_HEADS):
        kt[e] = jnp.transpose(kf[:, pl.ds(e * HEAD, HEAD)].astype(F32)).astype(BF)

    def dq_out(h):
        return pltpu.make_async_copy(
            qs.at[h // 8, pl.ds((h % 8) * ROWS, ROWS)], dq_hbm.at[:, pl.ds(h * HEAD, HEAD)], dq_s.at[0])

    def second(e, carry):
        for i in range(KV_HEADS):
            @pl.when(e == i)
            def _():
                landed(three(i), v_r.at[i])
                if i < 2:
                    v_send(i + 2)
        at_head(e, 2, g_step2)
        ecol = pl.ds(pl.multiple_of(e * HEAD, HEAD), HEAD)
        values_e = vf[:, ecol]
        for hh in range(8):
            rows = slice(hh * ROWS, (hh + 1) * ROWS)
            dp = nt(values_e, dos[e, rows, :])
            p = prob[e, :, rows].astype(F32)
            rd = jnp.sum(p * dp, axis=0, keepdims=True) * inv_row[e * 8 + hh]
            prob[e, :, rows] = (p * (dp - rd)).astype(BF)
        acc[:, ecol] = nn(prob[e], qs[e])
        dq_t = nn(kt[e], prob[e]) * SCALE
        for hh in range(8):
            rows = slice(hh * ROWS, (hh + 1) * ROWS)
            qs[e, rows, :] = jnp.transpose(dq_t[:, rows]).astype(BF)
        for hh in range(8):
            dq_out(e * 8 + hh).start()
        for i in range(KV_HEADS):
            at_head(e, i, lambda i=i: dk_start(i))
        return carry

    lax.fori_loop(0, KV_HEADS, second, 0)

    g_step3()
    dk_ref[...] = (dk_finish() * SCALE).astype(BF)
    g_step4()

    landed(qs, dq_s.at[0])
    landed(kf.at[pl.ds(0, 768)], k_s.at[0])
    landed(vf.at[pl.ds(0, 768)], v_s.at[0])
    l_done()
    a_done()
    b_done()
    give_part.wait_send()
    give_dvl.wait_send()

    landed(tok.at[pl.ds(ROWS, ROWS)], ts_sem.at[0])


def per_device(tokens, w, queries, keys, cotangent, block_dest, doc_ids):
    vm = lambda shape, t: pltpu.VMEM(shape, t)
    dma = lambda n: pltpu.SemaphoreType.DMA((n,))
    anyspec = pl.BlockSpec(memory_space=pl.ANY)
    vspec = pl.BlockSpec(memory_space=pltpu.VMEM)
    scratch = [
        vm((512, 4096), BF),
        vm((4, 4, 256, FEAT), BF),
        vm((KV_HEADS, 8 * ROWS, HEAD), BF),
        vm((KV_HEADS, 8 * ROWS, HEAD), BF),
        vm((KEYS, FEAT), BF),
        vm((KV_HEADS, HEAD, KEYS), BF),
        vm((KEYS, FEAT), BF),
        vm((KV_HEADS, KEYS, 8 * ROWS), BF),
        vm((HEADS, 1, ROWS), F32),
        vm((KEYS, ROWS), F32),
        vm((KEYS, FEAT), F32),
        vm((ROWS, FEAT), F32),
        vm((ROWS, FEAT), F32),
        vm((SLOTS, FEAT), BF),
        vm((SLOTS, FEAT), BF),
        vm((SLOTS, 128), BF),
        vm((SLOTS, 128), BF),
        vm((SLOTS, ROWS), BF),
        vm((SLOTS, ROWS), BF),
        vm((SLOTS, FEAT), BF),
        vm((SLOTS, FEAT), BF),
        vm((512, FEAT), BF),
        vm((KEYS, FEAT), BF),
        vm((3, ROWS, FEAT), BF),
        vm((2, 128, FEAT), BF),
        vm((2, 128, FEAT), BF),
        vm((2, 128, FEAT), BF),
        vm((2, 128, FEAT), BF),
        vm((4, 128, FEAT), BF),
        vm((4, 128, FEAT), BF),
        vm((4, 128, FEAT), BF),
        vm((4, 128, FEAT), BF),
        vm((3, 128, FEAT), BF),
        vm((3, 128, FEAT), BF),
        vm((3, 64, FEAT), BF),
        dma(2), dma(4), dma(4), dma(1), dma(1), dma(1),
        dma(1), dma(1), dma(1), dma(8), dma(1), dma(17), dma(1), dma(4),
        dma(1), dma(1), dma(1), dma(1), dma(1), dma(1),
        dma(1), dma(1), dma(1), dma(1),
        dma(1), dma(4), dma(1), dma(1), dma(1), dma(1),
        dma(1), dma(8), dma(1), dma(2), dma(1), dma(1), dma(1),
        pltpu.SemaphoreType.REGULAR,
    ]
    return pl.pallas_call(
        kernel,
        out_shape=(
            jax.ShapeDtypeStruct((ROWS, 4096), BF),
            jax.ShapeDtypeStruct((ROWS, FEAT), BF),
            jax.ShapeDtypeStruct((64, FEAT), F32),
        ),
        in_specs=[anyspec] * 5 + [pl.BlockSpec(memory_space=pltpu.SMEM), vspec],
        out_specs=(anyspec, vspec, vspec),
        scratch_shapes=scratch,
        compiler_params=pltpu.CompilerParams(
            collective_id=0, has_side_effects=True, vmem_limit_bytes=62 * 1024 * 1024
        ),
        name="attention_and_weights",
    )(tokens, w, queries, keys, cotangent, block_dest, doc_ids)


def solution(mesh):
    both = P(("dp", "sp"), None)
    return jax.shard_map(
        per_device,
        mesh=mesh,
        in_specs=(both, both, both, both, both, P(("dp", "sp")), P("dp", None)),
        out_specs=(both, both, both),
        check_vma=False,
    )
```

```python
import functools
import math

import jax
import jax.numpy as jnp
from jax import lax
from jax.experimental import pallas as pl
from jax.experimental.pallas import tpu as pltpu
from jax.sharding import PartitionSpec as P

MESH = pl.DeviceIdType.MESH
BF = jnp.bfloat16
F32 = jnp.float32
HEADS = 32
KV_HEADS = 4
HEAD = 128
ROWS = 256
KEYS = 1024
FEAT = 512
SLOTS = 512
BLK = 8
SCALE = 1.0 / math.sqrt(HEAD)
LOG2E = math.log2(math.e)


def nn(a, b):
    return lax.dot_general(a, b, (((1,), (0,)), ((), ())), preferred_element_type=F32)


def nt(a, b):
    return lax.dot_general(a, b, (((1,), (1,)), ((), ())), preferred_element_type=F32)


def tn(a, b):
    return lax.dot_general(a, b, (((0,), (0,)), ((), ())), preferred_element_type=F32)


def kernel(
    tok_hbm, w_hbm, q_hbm, k_hbm, do_hbm, dest_ref, doc_ref,
    dq_hbm, dk_ref, wg_ref,
    tok, wh, qs, dos, kf, kt, vf, prob, inv_row, bias, acc, part, part_in,
    snd, rcv, lsnd, lrcv, fwd, bwd_t, bsnd, brcv, dvl,
    gsend, gin, f1a, f2a, f1b, f2b, mpa, mma, mpb, mmb, s2a, s2b, s3,
    loc_sem, q_sem, do_sem, tl_sem, ts_sem, tr_sem, wx_s, wx_r, w2_s, w2_r, w3_s, w3_r, k_s, k_r,
    l_s, l_r, a_s, a_r, b_s, b_r, p_s, p_r, d_s, d_r, v_s, v_r, dv_s, dv_r, dk_s, dk_r,
    g_s, g_r, g2_s, g2_r, g3_s, g3_r, dq_s, relay,
):
    me = lax.axis_index("dp")
    x = lax.axis_index("sp")
    z, y, c = me // 8, (me // 2) % 4, me % 2

    def at(zz, yy, xx):
        return (zz * 8 + yy * 2 + c, xx)

    def up(v, o):
        return (v + o) % 4

    def along_x(o):
        return at(z, y, up(x, o))

    def along_y(o):
        return at(z, up(y, o), x)

    def along_z(o):
        return at(up(z, o), y, x)

    sibling = (z * 8 + y * 2 + (1 - c), x)

    def remote(src, dst, ss, rs, dev):
        return pltpu.make_async_remote_copy(src, dst, ss, rs, device_id=dev, device_id_type=MESH)

    def landed(ref, sem):
        pltpu.make_async_copy(ref, ref, sem).wait()

    own_w = pltpu.make_async_copy(w_hbm, wh.at[z, y, pl.ds(x * 64, 64)], loc_sem.at[0])
    own_k = pltpu.make_async_copy(k_hbm, kf.at[pl.ds(x * ROWS, ROWS)], loc_sem.at[1])

    def head_in(src, dst, sem, h):
        return pltpu.make_async_copy(
            src.at[:, pl.ds(h * HEAD, HEAD)], dst.at[h // 8, pl.ds((h % 8) * ROWS, ROWS)], sem.at[h // 8])

    def q_in(h):
        return head_in(q_hbm, qs, q_sem, h)

    def do_in(h):
        return head_in(do_hbm, dos, do_sem, h)

    def tok_local(i):
        return pltpu.make_async_copy(
            tok_hbm.at[:, pl.ds((i * 2 + c) * 256, 256)],
            tok.at[pl.ds(0, ROWS), pl.ds(i * 256, 256)], tl_sem.at[0])

    def tok_remote(i):
        return remote(
            tok_hbm.at[:, pl.ds((i * 2 + 1 - c) * 256, 256)],
            tok.at[pl.ds(ROWS, ROWS), pl.ds(i * 256, 256)], ts_sem.at[0], tr_sem.at[0], sibling)

    barrier = pltpu.get_barrier_semaphore()

    for o in (1, 2, 3):
        across = (up(z, o) * 8 + y * 2 + (1 - c), x)
        for partner in (along_x(o), along_y(o), along_z(o), across):
            pl.semaphore_signal(barrier, inc=1, device_id=partner, device_id_type=MESH)
    pl.semaphore_signal(barrier, inc=1, device_id=sibling, device_id_type=MESH)
    own_k.start()
    own_w.start()

    def heads_in(h, carry):
        q_in(h).start()
        do_in(h).start()
        return carry

    lax.fori_loop(0, HEADS, heads_in, 0)

    cut = jnp.sum(jnp.where(doc_ref[0:1, :] == 0, 1, 0), axis=1, keepdims=True)
    k_pos = lax.broadcasted_iota(jnp.int32, (KEYS, ROWS), 0)
    q_pos = lax.broadcasted_iota(jnp.int32, (KEYS, ROWS), 1) + x * ROWS
    allowed = (k_pos <= q_pos) & ((k_pos < cut) == (q_pos < cut))
    bias[...] = jnp.where(allowed, 0.0, -1e30)

    blk = lax.broadcasted_iota(jnp.int32, (8, ROWS), 1) // BLK
    dest = jnp.zeros((8, ROWS), jnp.int32)
    for b in range(32):
        dest = jnp.where(blk == b, dest_ref[b], dest)
    dest_dp, target = dest // 128, dest % 32
    rank = jnp.zeros((8, ROWS), jnp.int32)
    for b in range(31):
        rank = rank + jnp.where((blk > b) & (dest_dp == dest_ref[b] // 128), 1, 0)
    pos = (dest_dp * 2 + rank)[0:1, :]
    r_i = lax.broadcasted_iota(jnp.int32, (SLOTS, ROWS), 0)
    c_i = lax.broadcasted_iota(jnp.int32, (SLOTS, ROWS), 1)
    same_row = (r_i % BLK) == (c_i % BLK)
    fwd[...] = jnp.where(same_row & ((r_i // BLK) == pos), 1.0, 0.0).astype(BF)
    lab_rows = jnp.broadcast_to((target + 1).astype(F32)[0:1, :], (HEAD, ROWS))
    lsnd[...] = nn(fwd[...], jnp.transpose(lab_rows).astype(BF)).astype(BF)
    pl.semaphore_wait(barrier, 13)
    for o in (1, 2, 3):
        pl.semaphore_signal(relay, inc=1, device_id=along_y(o), device_id_type=MESH)

    def w_x(o):
        return remote(w_hbm, wh.at[z, y, pl.ds(x * 64, 64)], wx_s.at[0], wx_r.at[0], along_x(o))

    def k_x(o, e):
        cols = pl.ds(e * HEAD, HEAD)
        return remote(k_hbm.at[:, cols], kf.at[pl.ds(x * ROWS, ROWS), cols], k_s.at[0], k_r.at[e], along_x(o))

    for o in (1, 3, 2):
        w_x(o).start()
    for o in (1, 3, 2):
        k_x(o, 0).start()

    def peers(send_buf, recv_buf, ss, rs):
        def one(o):
            p = (me + o) % 32
            return remote(send_buf.at[pl.ds(p * 16, 16)], recv_buf.at[pl.ds(me * 16, 16)], ss.at[0], rs.at[0], (p, x))

        def start():
            def body(o, carry):
                one(o).start()
                return carry

            lax.fori_loop(1, 32, body, 0)
            mine = pl.ds(pl.multiple_of(me * 16, 16), 16)
            recv_buf[mine, :] = send_buf[mine, :]

        def wait_recv():
            landed(recv_buf.at[pl.ds(0, 496)], rs.at[0])

        def wait_send():
            landed(send_buf.at[pl.ds(0, 496)], ss.at[0])

        return start, wait_recv, wait_send

    l_start, l_recv, l_done = peers(lsnd, lrcv, l_s, l_r)
    a_start, a_recv, a_done = peers(snd, rcv, a_s, a_r)
    b_start, b_recv, b_done = peers(bsnd, brcv, b_s, b_r)

    def start_tokens(i, carry):
        tok_local(i).start()
        tok_remote(i).start()
        return carry


    def w_2a(o):
        blk = wh.at[z, y, pl.ds(0, 128)]
        return remote(blk, blk, w2_s.at[0], w2_r.at[o], along_y(o))

    def w_2b(o):
        blk = wh.at[z, y, pl.ds(128, 128)]
        return remote(blk, blk, w2_s.at[0], w2_r.at[4 + o], along_z(o))

    def w_3a(j, m):
        yy = up(y, j)
        if m < 2:
            blk = wh.at[z, yy, pl.ds(0, 128)]
        elif m == 2:
            blk = wh.at[up(z, 3), yy, pl.ds(0, 64)]
        else:
            blk = wh.at[up(z, 1), yy, pl.ds(64, 64)]
        i = j * 2 + m if m < 2 else 16
        return remote(blk, blk, w3_s.at[0], w3_r.at[i], along_z(1 if m % 2 == 0 else 3))

    def w_3b(j, m):
        zz = up(z, j)
        if m < 2:
            blk = wh.at[zz, y, pl.ds(128, 128)]
        elif m == 2:
            blk = wh.at[zz, up(y, 3), pl.ds(128, 64)]
        else:
            blk = wh.at[zz, up(y, 1), pl.ds(192, 64)]
        i = 8 + j * 2 + m if m < 2 else 16
        return remote(blk, blk, w3_s.at[0], w3_r.at[i], along_y(1 if m % 2 == 0 else 3))

    def w_begin():
        own_w.wait()
        landed(wh.at[0, 0, pl.ds(0, 192)], wx_r.at[0])
        for o in (1, 3, 2):
            w_2a(o).start()
            w_2b(o).start()
        for m in (0, 1):
            w_3a(0, m).start()
            w_3b(0, m).start()

    def w_full(j):
        w_2a((4 - j) % 4).wait_recv()
        w_2b((4 - j) % 4).wait_recv()
        for m in (0, 1):
            w_3a(j, m).start()
            w_3b(j, m).start()

    def w_forward(j):
        for m in (0, 1):
            w_3a(j, m).wait_recv()
            w_3a(j, m + 2).start()
            w_3b(j, m).wait_recv()
            w_3b(j, m + 2).start()

    def w_end():
        landed(wh.at[0], w3_r.at[16])
        landed(wh.at[0, 0, pl.ds(0, 192)], wx_s.at[0])
        landed(wh.at[0, pl.ds(0, 3)], w2_s.at[0])
        landed(wh.at[pl.ds(0, 3)], w3_s.at[0])

    def sum_x(ss, rs):
        def one(o, e):
            cols = pl.ds(e * HEAD, HEAD)
            return remote(gsend.at[pl.ds(up(x, o) * ROWS, ROWS), cols], gin.at[o - 1, :, cols], ss.at[0], rs.at[0], along_x(o))

        def start(e):
            cols = pl.ds(e * HEAD, HEAD)
            gsend[:, cols] = acc[:, cols].astype(BF)
            for o in (1, 3, 2):
                one(o, e).start()

        def finish():
            landed(gin, rs.at[0])
            own = acc[pl.ds(pl.multiple_of(x * ROWS, ROWS), ROWS), :]
            total = own + gin[0].astype(F32) + gin[1].astype(F32) + gin[2].astype(F32)
            landed(gin, ss.at[0])
            return total

        return start, finish

    dv_start, dv_finish = sum_x(dv_s, dv_r)
    dk_start, dk_finish = sum_x(dk_s, dk_r)

    def at_head(h, where, act):
        pl.when(h == where)(act)

    own_k.wait()

    def three(e):
        return kf.at[pl.ds(0, 768), pl.ds(e * HEAD, HEAD)]

    def k_send(e):
        for o in (1, 3, 2):
            k_x(o, e).start()

    def w_rest():
        for j in (1, 3, 2):
            w_full(j)
        w_forward(0)

    w_begin()
    k_send(1)
    k_send(2)
    pl.semaphore_wait(relay, 3)
    l_start()
    lax.fori_loop(0, 16, start_tokens, 0)

    def first(e, carry):
        for i in range(KV_HEADS):
            @pl.when(e == i)
            def _():
                landed(three(i), k_r.at[i])
                if i == 1:
                    k_send(3)
        at_head(e, 2, w_rest)
        at_head(e, 3, lambda: w_forward(1))
        landed(qs.at[e], q_sem.at[e])
        landed(dos.at[e], do_sem.at[e])
        ecol = pl.ds(pl.multiple_of(e * HEAD, HEAD), HEAD)
        keys = kf[:, ecol]
        for hh in range(8):
            rows = slice(hh * ROWS, (hh + 1) * ROWS)
            s = nt(keys, qs[e, rows, :]) * (SCALE * LOG2E) + bias[...]
            m = jnp.max(s, axis=0, keepdims=True)
            p = jnp.exp2(s - m)
            inv = 1.0 / jnp.sum(p, axis=0, keepdims=True)
            prob[e, :, rows] = p.astype(BF)
            inv_row[e * 8 + hh] = inv
            inv_rows = jnp.transpose(jnp.broadcast_to(inv, (HEAD, ROWS)))
            dos[e, rows, :] = (dos[e, rows, :].astype(F32) * inv_rows).astype(BF)
        acc[:, ecol] = nn(prob[e], dos[e])
        for i in range(KV_HEADS):
            at_head(e, i, lambda i=i: dv_start(i))
        return carry

    lax.fori_loop(0, KV_HEADS, first, 0)
    w_forward(3)
    l_recv()
    lab = lrcv[...].astype(F32)
    want = (c_i // BLK + 1).astype(F32)
    bwd_t[...] = jnp.where(same_row & (jnp.concatenate([lab, lab], axis=1) == want), 1.0, 0.0).astype(BF)
    w_forward(2)

    bsnd[...] = nn(bwd_t[...], dv_finish().astype(BF)).astype(BF)
    b_start()

    landed(tok.at[pl.ds(0, ROWS)], tl_sem.at[0])
    landed(tok.at[pl.ds(ROWS, ROWS)], tr_sem.at[0])

    def project(rows, blocks):
        total = None
        for dz, dy in blocks:
            zz, yy = up(z, dz), up(y, dy)
            cols = pl.ds(pl.multiple_of((zz * 4 + yy) * 256, 256), 256)
            term = nn(tok[rows, cols], wh[zz, yy])
            total = term if total is None else total + term
        return total

    near = [(dz, dy) for dz in (0, 1, 3) for dy in (0, 1, 3)]
    far = [(2, dy) for dy in range(4)] + [(dz, 2) for dz in (0, 1, 3)]
    part[...] = project(pl.ds(0, 512), near)
    w_end()


    give_part = remote(part.at[pl.ds(ROWS, ROWS)], part_in, p_s.at[0], p_r.at[0], sibling)
    part[pl.ds(ROWS, ROWS), :] += project(pl.ds(ROWS, ROWS), far)
    give_part.start()
    mine = part[pl.ds(0, ROWS), :] + project(pl.ds(0, ROWS), far)
    give_part.wait_recv()
    values = (mine + part_in[...]).astype(BF)
    snd[...] = nn(fwd[...], values).astype(BF)
    a_start()

    b_recv()
    dvl[pl.ds(0, ROWS), :] = tn(fwd[...], brcv[...]).astype(BF)
    give_dvl = remote(dvl.at[pl.ds(0, ROWS)], dvl.at[pl.ds(ROWS, ROWS)], d_s.at[0], d_r.at[0], sibling)
    give_dvl.start()
    give_dvl.wait_recv()

    def weight_blocks(i, carry):
        for n in range(8):
            cols = pl.ds(pl.multiple_of(i * 2048 + n * 256, 256), 256)
            wh[i * 2 + n // 4, n % 4] = tn(tok[:, cols], dvl[...]).astype(BF)
        return carry

    lax.fori_loop(0, 2, weight_blocks, 0)

    a_rows, b_rows = pl.ds(0, 128), pl.ds(128, 128)
    low2, high2 = pl.ds(0, 2), pl.ds(2, 2)

    g_1 = [
        remote(wh.at[up(z, 2), low2, a_rows], f1a, g_s.at[0], g_r.at[0], along_z(1)),
        remote(wh.at[up(z, 2), high2, a_rows], f2a, g_s.at[0], g_r.at[1], along_z(3)),
        remote(wh.at[low2, up(y, 2), b_rows], f1b, g_s.at[0], g_r.at[2], along_y(1)),
        remote(wh.at[high2, up(y, 2), b_rows], f2b, g_s.at[0], g_r.at[3], along_y(3)),
        remote(wh.at[up(z, 1), high2, a_rows], mpa.at[high2], g_s.at[0], g_r.at[4], along_z(1)),
        remote(wh.at[up(z, 3), low2, a_rows], mma.at[low2], g_s.at[0], g_r.at[5], along_z(3)),
        remote(wh.at[high2, up(y, 1), b_rows], mpb.at[high2], g_s.at[0], g_r.at[6], along_y(1)),
        remote(wh.at[low2, up(y, 3), b_rows], mmb.at[low2], g_s.at[0], g_r.at[7], along_y(3)),
    ]
    g_2 = [
        remote(wh.at[up(z, 1), low2, a_rows], mpa.at[low2], g_s.at[0], g_r.at[4], along_z(1)),
        remote(wh.at[up(z, 3), high2, a_rows], mma.at[high2], g_s.at[0], g_r.at[5], along_z(3)),
        remote(wh.at[low2, up(y, 1), b_rows], mpb.at[low2], g_s.at[0], g_r.at[6], along_y(1)),
        remote(wh.at[high2, up(y, 3), b_rows], mmb.at[high2], g_s.at[0], g_r.at[7], along_y(3)),
    ]

    def g_3a(o):
        return remote(wh.at[z, up(y, o), a_rows], s2a.at[o - 1], g2_s.at[0], g2_r.at[0], along_y(o))

    def g_3b(o):
        return remote(wh.at[up(z, o), y, b_rows], s2b.at[o - 1], g2_s.at[0], g2_r.at[1], along_z(o))

    def g_x(o):
        rows = pl.ds(up(x, o) * 64, 64)
        return remote(wh.at[z, y, rows], s3.at[o - 1], g3_s.at[0], g3_r.at[0], along_x(o))

    def bsum(*terms):
        total = terms[0].astype(F32)
        for t in terms[1:]:
            total = total + t.astype(F32)
        return total

    def g_step1():
        for i in range(4):
            g_1[i].wait_recv()
            if i == 0:
                wh[up(z, 1), 0:2, 0:128] = bsum(wh[up(z, 1), 0:2, 0:128], f1a[...]).astype(BF)
            elif i == 1:
                wh[up(z, 3), 2:4, 0:128] = bsum(wh[up(z, 3), 2:4, 0:128], f2a[...]).astype(BF)
            elif i == 2:
                wh[0:2, up(y, 1), 128:256] = bsum(wh[0:2, up(y, 1), 128:256], f1b[...]).astype(BF)
            else:
                wh[2:4, up(y, 3), 128:256] = bsum(wh[2:4, up(y, 3), 128:256], f2b[...]).astype(BF)
            g_2[i].start()

    def g_step2():
        for i, buf in enumerate((mpa, mma, mpb, mmb)):
            landed(buf, g_r.at[4 + i])
        for i in range(4):
            wh[z, i, 0:128] = bsum(wh[z, i, 0:128], mpa[i], mma[i]).astype(BF)
            wh[i, y, 128:256] = bsum(wh[i, y, 128:256], mpb[i], mmb[i]).astype(BF)
        for o in (1, 3, 2):
            g_3a(o).start()
            g_3b(o).start()

    def g_step3():
        landed(s2a, g2_r.at[0])
        landed(s2b, g2_r.at[1])
        wh[z, y, 0:128] = bsum(wh[z, y, 0:128], s2a[0], s2a[1], s2a[2]).astype(BF)
        wh[z, y, 128:256] = bsum(wh[z, y, 128:256], s2b[0], s2b[1], s2b[2]).astype(BF)
        for o in (1, 3, 2):
            g_x(o).start()

    def g_step4():
        landed(s3, g3_r.at[0])
        rows = pl.ds(pl.multiple_of(x * 64, 64), 64)
        wg_ref[...] = bsum(wh[z, y, rows, :], s3[0], s3[1], s3[2])
        landed(wh.at[pl.ds(0, 3)], g_s.at[0])
        landed(wh.at[0, pl.ds(0, 3)], g2_s.at[0])
        landed(s3, g3_s.at[0])

    for d in g_1[:4]:
        d.start()

    a_recv()
    mine_rows = pl.ds(pl.multiple_of(x * ROWS, ROWS), ROWS)
    vf[mine_rows, :] = tn(bwd_t[...], rcv[...]).astype(BF)

    def v_x(o, e):
        blk = vf.at[pl.ds(x * ROWS, ROWS), pl.ds(e * HEAD, HEAD)]
        return remote(blk, blk, v_s.at[0], v_r.at[e], along_x(o))

    def v_send(e):
        for o in (1, 3, 2):
            v_x(o, e).start()

    v_send(0)
    for d in g_1[4:]:
        d.start()
    v_send(1)
    for e in range(KV_HEADS):
        kt[e] = jnp.transpose(kf[:, pl.ds(e * HEAD, HEAD)].astype(F32)).astype(BF)

    def dq_out(h):
        return pltpu.make_async_copy(
            qs.at[h // 8, pl.ds((h % 8) * ROWS, ROWS)], dq_hbm.at[:, pl.ds(h * HEAD, HEAD)], dq_s.at[0])

    def second(e, carry):
        for i in range(KV_HEADS):
            @pl.when(e == i)
            def _():
                landed(three(i), v_r.at[i])
                if i < 2:
                    v_send(i + 2)
        at_head(e, 1, g_step1)
        at_head(e, 3, g_step2)
        ecol = pl.ds(pl.multiple_of(e * HEAD, HEAD), HEAD)
        values_e = vf[:, ecol]
        for hh in range(8):
            rows = slice(hh * ROWS, (hh + 1) * ROWS)
            dp = nt(values_e, dos[e, rows, :])
            p = prob[e, :, rows].astype(F32)
            rd = jnp.sum(p * dp, axis=0, keepdims=True) * inv_row[e * 8 + hh]
            prob[e, :, rows] = (p * (dp - rd)).astype(BF)
        acc[:, ecol] = nn(prob[e], qs[e])
        dq_t = nn(kt[e], prob[e]) * SCALE
        for hh in range(8):
            rows = slice(hh * ROWS, (hh + 1) * ROWS)
            qs[e, rows, :] = jnp.transpose(dq_t[:, rows]).astype(BF)
        for hh in range(8):
            dq_out(e * 8 + hh).start()
        for i in range(KV_HEADS):
            at_head(e, i, lambda i=i: dk_start(i))
        return carry

    lax.fori_loop(0, KV_HEADS, second, 0)

    g_step3()
    dk_ref[...] = (dk_finish() * SCALE).astype(BF)
    g_step4()

    landed(qs, dq_s.at[0])
    landed(kf.at[pl.ds(0, 768)], k_s.at[0])
    landed(vf.at[pl.ds(0, 768)], v_s.at[0])
    l_done()
    a_done()
    b_done()
    give_part.wait_send()
    give_dvl.wait_send()

    landed(tok.at[pl.ds(ROWS, ROWS)], ts_sem.at[0])


def hand_on(dq_in, dk_in, wg_in, dq_out, dk_out, wg_out, dq_v, dk_v, wg_v, sem):
    steps = [(dk_in, dk_v, dk_out), (wg_in, wg_v, wg_out)]
    for i in range(8):
        rows = pl.ds(i * 32, 32)
        steps.append((dq_in.at[rows], dq_v.at[rows], dq_out.at[rows]))
    into = [pltpu.make_async_copy(a, v, sem.at[0, i]) for i, (a, v, _) in enumerate(steps)]
    away = [pltpu.make_async_copy(v, b, sem.at[1, i]) for i, (_, v, b) in enumerate(steps)]
    for copy in into:
        copy.start()
    for i, copy in enumerate(into):
        copy.wait()
        away[i].start()
    for copy in away:
        copy.wait()


def per_device(tokens, w, queries, keys, cotangent, block_dest, doc_ids):
    vm = lambda shape, t: pltpu.VMEM(shape, t)
    dma = lambda n: pltpu.SemaphoreType.DMA((n,))
    anyspec = pl.BlockSpec(memory_space=pl.ANY)
    vspec = pl.BlockSpec(memory_space=pltpu.VMEM)
    scratch = [
        vm((512, 4096), BF),
        vm((4, 4, 256, FEAT), BF),
        vm((KV_HEADS, 8 * ROWS, HEAD), BF),
        vm((KV_HEADS, 8 * ROWS, HEAD), BF),
        vm((KEYS, FEAT), BF),
        vm((KV_HEADS, HEAD, KEYS), BF),
        vm((KEYS, FEAT), BF),
        vm((KV_HEADS, KEYS, 8 * ROWS), BF),
        vm((HEADS, 1, ROWS), F32),
        vm((KEYS, ROWS), F32),
        vm((KEYS, FEAT), F32),
        vm((2 * ROWS, FEAT), F32),
        vm((ROWS, FEAT), F32),
        vm((SLOTS, FEAT), BF),
        vm((SLOTS, FEAT), BF),
        vm((SLOTS, 128), BF),
        vm((SLOTS, 128), BF),
        vm((SLOTS, ROWS), BF),
        vm((SLOTS, ROWS), BF),
        vm((SLOTS, FEAT), BF),
        vm((SLOTS, FEAT), BF),
        vm((512, FEAT), BF),
        vm((KEYS, FEAT), BF),
        vm((3, ROWS, FEAT), BF),
        vm((2, 128, FEAT), BF),
        vm((2, 128, FEAT), BF),
        vm((2, 128, FEAT), BF),
        vm((2, 128, FEAT), BF),
        vm((4, 128, FEAT), BF),
        vm((4, 128, FEAT), BF),
        vm((4, 128, FEAT), BF),
        vm((4, 128, FEAT), BF),
        vm((3, 128, FEAT), BF),
        vm((3, 128, FEAT), BF),
        vm((3, 64, FEAT), BF),
        dma(2), dma(4), dma(4), dma(1), dma(1), dma(1),
        dma(1), dma(1), dma(1), dma(8), dma(1), dma(17), dma(1), dma(4),
        dma(1), dma(1), dma(1), dma(1), dma(1), dma(1),
        dma(1), dma(1), dma(1), dma(1),
        dma(1), dma(4), dma(1), dma(1), dma(1), dma(1),
        dma(1), dma(8), dma(1), dma(2), dma(1), dma(1), dma(1),
        pltpu.SemaphoreType.REGULAR,
    ]
    raw = pl.pallas_call(
        kernel,
        out_shape=(
            jax.ShapeDtypeStruct((ROWS, 4096), BF),
            jax.ShapeDtypeStruct((ROWS, FEAT), BF),
            jax.ShapeDtypeStruct((64, FEAT), F32),
        ),
        in_specs=[anyspec] * 5 + [pl.BlockSpec(memory_space=pltpu.SMEM), vspec],
        out_specs=(anyspec, vspec, vspec),
        scratch_shapes=scratch,
        compiler_params=pltpu.CompilerParams(
            collective_id=0, has_side_effects=True, vmem_limit_bytes=62 * 1024 * 1024
        ),
        name="attention_and_weights",
    )(tokens, w, queries, keys, cotangent, block_dest, doc_ids)
    return pl.pallas_call(
        hand_on,
        out_shape=tuple(jax.ShapeDtypeStruct(r.shape, r.dtype) for r in raw),
        in_specs=[anyspec] * 3,
        out_specs=(anyspec,) * 3,
        scratch_shapes=[
            vm((ROWS, 4096), BF), vm((ROWS, FEAT), BF), vm((64, FEAT), F32), pltpu.SemaphoreType.DMA((2, 10))],
        name="hand_on",
    )(*raw)


def solution(mesh):
    both = P(("dp", "sp"), None)
    return jax.shard_map(
        per_device,
        mesh=mesh,
        in_specs=(both, both, both, both, both, P(("dp", "sp")), P("dp", None)),
        out_specs=(both, both, both),
        check_vma=False,
    )
```

```python
import functools
import math

import jax
import jax.numpy as jnp
from jax import lax
from jax.experimental import pallas as pl
from jax.experimental.pallas import tpu as pltpu
from jax.sharding import PartitionSpec as P

MESH = pl.DeviceIdType.MESH
BF = jnp.bfloat16
F32 = jnp.float32
HEADS = 32
KV_HEADS = 4
HEAD = 128
ROWS = 256
KEYS = 1024
FEAT = 512
SLOTS = 512
BLK = 8
SCALE = 1.0 / math.sqrt(HEAD)
LOG2E = math.log2(math.e)


def nn(a, b):
    return lax.dot_general(a, b, (((1,), (0,)), ((), ())), preferred_element_type=F32)


def nt(a, b):
    return lax.dot_general(a, b, (((1,), (1,)), ((), ())), preferred_element_type=F32)


def tn(a, b):
    return lax.dot_general(a, b, (((0,), (0,)), ((), ())), preferred_element_type=F32)


def kernel(
    tok_hbm, w_hbm, q_hbm, k_hbm, do_hbm, dest_ref, doc_ref,
    dq_hbm, dk_ref, wg_ref,
    tok, wh, qs, dos, kf, kt, vf, prob, inv_row, bias, acc, part, part_in,
    snd, rcv, lsnd, lrcv, fwd, bwd_t, bsnd, brcv, dvl,
    gsend, gin, f1a, f2a, f1b, f2b, mpa, mma, mpb, mmb, s2a, s2b, s3,
    loc_sem, q_sem, do_sem, tl_sem, ts_sem, tr_sem, wx_s, wx_r, w2_s, w2_r, w3_s, w3_r, k_s, k_r,
    l_s, l_r, a_s, a_r, b_s, b_r, p_s, p_r, d_s, d_r, v_s, v_r, dv_s, dv_r, dk_s, dk_r,
    g_s, g_r, g2_s, g2_r, g3_s, g3_r, dq_s, relay,
):
    me = lax.axis_index("dp")
    x = lax.axis_index("sp")
    z, y, c = me // 8, (me // 2) % 4, me % 2

    def at(zz, yy, xx):
        return (zz * 8 + yy * 2 + c, xx)

    def up(v, o):
        return (v + o) % 4

    def along_x(o):
        return at(z, y, up(x, o))

    def along_y(o):
        return at(z, up(y, o), x)

    def along_z(o):
        return at(up(z, o), y, x)

    sibling = (z * 8 + y * 2 + (1 - c), x)

    def remote(src, dst, ss, rs, dev):
        return pltpu.make_async_remote_copy(src, dst, ss, rs, device_id=dev, device_id_type=MESH)

    def landed(ref, sem):
        pltpu.make_async_copy(ref, ref, sem).wait()

    own_w = pltpu.make_async_copy(w_hbm, wh.at[z, y, pl.ds(x * 64, 64)], loc_sem.at[0])
    own_k = pltpu.make_async_copy(k_hbm, kf.at[pl.ds(x * ROWS, ROWS)], loc_sem.at[1])

    def head_in(src, dst, sem, h):
        return pltpu.make_async_copy(
            src.at[:, pl.ds(h * HEAD, HEAD)], dst.at[h // 8, pl.ds((h % 8) * ROWS, ROWS)], sem.at[h // 8])

    def q_in(h):
        return head_in(q_hbm, qs, q_sem, h)

    def do_in(h):
        return head_in(do_hbm, dos, do_sem, h)

    def tok_local(i):
        return pltpu.make_async_copy(
            tok_hbm.at[:, pl.ds((i * 2 + c) * 256, 256)],
            tok.at[pl.ds(0, ROWS), pl.ds(i * 256, 256)], tl_sem.at[0])

    def tok_remote(i):
        return remote(
            tok_hbm.at[:, pl.ds((i * 2 + 1 - c) * 256, 256)],
            tok.at[pl.ds(ROWS, ROWS), pl.ds(i * 256, 256)], ts_sem.at[0], tr_sem.at[0], sibling)

    barrier = pltpu.get_barrier_semaphore()

    for o in (1, 2, 3):
        across = (up(z, o) * 8 + y * 2 + (1 - c), x)
        for partner in (along_x(o), along_y(o), along_z(o), across):
            pl.semaphore_signal(barrier, inc=1, device_id=partner, device_id_type=MESH)
    pl.semaphore_signal(barrier, inc=1, device_id=sibling, device_id_type=MESH)
    own_k.start()
    own_w.start()

    def heads_in(h, carry):
        q_in(h).start()
        do_in(h).start()
        return carry

    lax.fori_loop(0, HEADS, heads_in, 0)

    cut = jnp.sum(jnp.where(doc_ref[0:1, :] == 0, 1, 0), axis=1, keepdims=True)
    k_pos = lax.broadcasted_iota(jnp.int32, (KEYS, ROWS), 0)
    q_pos = lax.broadcasted_iota(jnp.int32, (KEYS, ROWS), 1) + x * ROWS
    allowed = (k_pos <= q_pos) & ((k_pos < cut) == (q_pos < cut))
    bias[...] = jnp.where(allowed, 0.0, -1e30)

    blk = lax.broadcasted_iota(jnp.int32, (8, ROWS), 1) // BLK
    dest = jnp.zeros((8, ROWS), jnp.int32)
    for b in range(32):
        dest = jnp.where(blk == b, dest_ref[b], dest)
    dest_dp, target = dest // 128, dest % 32
    rank = jnp.zeros((8, ROWS), jnp.int32)
    for b in range(31):
        rank = rank + jnp.where((blk > b) & (dest_dp == dest_ref[b] // 128), 1, 0)
    pos = (dest_dp * 2 + rank)[0:1, :]
    r_i = lax.broadcasted_iota(jnp.int32, (SLOTS, ROWS), 0)
    c_i = lax.broadcasted_iota(jnp.int32, (SLOTS, ROWS), 1)
    same_row = (r_i % BLK) == (c_i % BLK)
    fwd[...] = jnp.where(same_row & ((r_i // BLK) == pos), 1.0, 0.0).astype(BF)
    lab_rows = jnp.broadcast_to((target + 1).astype(F32)[0:1, :], (HEAD, ROWS))
    lsnd[...] = nn(fwd[...], jnp.transpose(lab_rows).astype(BF)).astype(BF)
    pl.semaphore_wait(barrier, 13)
    for o in (1, 2, 3):
        pl.semaphore_signal(relay, inc=1, device_id=along_y(o), device_id_type=MESH)

    def w_x(o):
        return remote(w_hbm, wh.at[z, y, pl.ds(x * 64, 64)], wx_s.at[0], wx_r.at[0], along_x(o))

    def k_x(o, e):
        cols = pl.ds(e * HEAD, HEAD)
        return remote(k_hbm.at[:, cols], kf.at[pl.ds(x * ROWS, ROWS), cols], k_s.at[0], k_r.at[e], along_x(o))

    for o in (1, 3, 2):
        w_x(o).start()
    for o in (1, 3, 2):
        k_x(o, 0).start()

    def peers(send_buf, recv_buf, ss, rs):
        def one(o):
            p = (me + o) % 32
            return remote(send_buf.at[pl.ds(p * 16, 16)], recv_buf.at[pl.ds(me * 16, 16)], ss.at[0], rs.at[0], (p, x))

        def start():
            def body(o, carry):
                one(o).start()
                return carry

            lax.fori_loop(1, 32, body, 0)
            mine = pl.ds(pl.multiple_of(me * 16, 16), 16)
            recv_buf[mine, :] = send_buf[mine, :]

        def wait_recv():
            landed(recv_buf.at[pl.ds(0, 496)], rs.at[0])

        def wait_send():
            landed(send_buf.at[pl.ds(0, 496)], ss.at[0])

        return start, wait_recv, wait_send

    l_start, l_recv, l_done = peers(lsnd, lrcv, l_s, l_r)
    a_start, a_recv, a_done = peers(snd, rcv, a_s, a_r)
    b_start, b_recv, b_done = peers(bsnd, brcv, b_s, b_r)

    def start_tokens(i, carry):
        tok_local(i).start()
        tok_remote(i).start()
        return carry


    def w_2a(o):
        blk = wh.at[z, y, pl.ds(0, 128)]
        return remote(blk, blk, w2_s.at[0], w2_r.at[o], along_y(o))

    def w_2b(o):
        blk = wh.at[z, y, pl.ds(128, 128)]
        return remote(blk, blk, w2_s.at[0], w2_r.at[4 + o], along_z(o))

    def w_3a(j, m):
        yy = up(y, j)
        if m < 2:
            blk = wh.at[z, yy, pl.ds(0, 128)]
        elif m == 2:
            blk = wh.at[up(z, 3), yy, pl.ds(0, 64)]
        else:
            blk = wh.at[up(z, 1), yy, pl.ds(64, 64)]
        i = j * 2 + m if m < 2 else 16
        return remote(blk, blk, w3_s.at[0], w3_r.at[i], along_z(1 if m % 2 == 0 else 3))

    def w_3b(j, m):
        zz = up(z, j)
        if m < 2:
            blk = wh.at[zz, y, pl.ds(128, 128)]
        elif m == 2:
            blk = wh.at[zz, up(y, 3), pl.ds(128, 64)]
        else:
            blk = wh.at[zz, up(y, 1), pl.ds(192, 64)]
        i = 8 + j * 2 + m if m < 2 else 16
        return remote(blk, blk, w3_s.at[0], w3_r.at[i], along_y(1 if m % 2 == 0 else 3))

    def w_begin():
        own_w.wait()
        landed(wh.at[0, 0, pl.ds(0, 192)], wx_r.at[0])
        for o in (1, 3, 2):
            w_2a(o).start()
            w_2b(o).start()
        for m in (0, 1):
            w_3a(0, m).start()
            w_3b(0, m).start()

    def w_full(j):
        w_2a((4 - j) % 4).wait_recv()
        w_2b((4 - j) % 4).wait_recv()
        for m in (0, 1):
            w_3a(j, m).start()
            w_3b(j, m).start()

    def w_forward(j):
        for m in (0, 1):
            w_3a(j, m).wait_recv()
            w_3a(j, m + 2).start()
            w_3b(j, m).wait_recv()
            w_3b(j, m + 2).start()

    def w_end():
        landed(wh.at[0], w3_r.at[16])
        landed(wh.at[0, 0, pl.ds(0, 192)], wx_s.at[0])
        landed(wh.at[0, pl.ds(0, 3)], w2_s.at[0])
        landed(wh.at[pl.ds(0, 3)], w3_s.at[0])

    def sum_x(ss, rs):
        def one(o, e):
            cols = pl.ds(e * HEAD, HEAD)
            return remote(gsend.at[pl.ds(up(x, o) * ROWS, ROWS), cols], gin.at[o - 1, :, cols], ss.at[0], rs.at[0], along_x(o))

        def start(e):
            cols = pl.ds(e * HEAD, HEAD)
            gsend[:, cols] = acc[:, cols].astype(BF)
            for o in (1, 3, 2):
                one(o, e).start()

        def finish():
            landed(gin, rs.at[0])
            own = acc[pl.ds(pl.multiple_of(x * ROWS, ROWS), ROWS), :]
            total = own + gin[0].astype(F32) + gin[1].astype(F32) + gin[2].astype(F32)
            landed(gin, ss.at[0])
            return total

        return start, finish

    dv_start, dv_finish = sum_x(dv_s, dv_r)
    dk_start, dk_finish = sum_x(dk_s, dk_r)

    def at_head(h, where, act):
        pl.when(h == where)(act)

    own_k.wait()

    def three(e):
        return kf.at[pl.ds(0, 768), pl.ds(e * HEAD, HEAD)]

    def k_send(e):
        for o in (1, 3, 2):
            k_x(o, e).start()

    def w_rest():
        for j in (1, 3, 2):
            w_full(j)
        w_forward(0)

    w_begin()
    k_send(1)
    k_send(2)
    pl.semaphore_wait(relay, 3)
    l_start()
    lax.fori_loop(0, 16, start_tokens, 0)

    def first(e, carry):
        for i in range(KV_HEADS):
            @pl.when(e == i)
            def _():
                landed(three(i), k_r.at[i])
                if i == 1:
                    k_send(3)
        at_head(e, 1, lambda: w_full(1))
        @pl.when(e == 2)
        def _():
            w_full(3)
            w_full(2)
            w_forward(0)
        at_head(e, 3, lambda: w_forward(1))
        landed(qs.at[e], q_sem.at[e])
        landed(dos.at[e], do_sem.at[e])
        ecol = pl.ds(pl.multiple_of(e * HEAD, HEAD), HEAD)
        keys = kf[:, ecol]
        for hh in range(8):
            rows = slice(hh * ROWS, (hh + 1) * ROWS)
            s = nt(keys, qs[e, rows, :]) * (SCALE * LOG2E) + bias[...]
            m = jnp.max(s, axis=0, keepdims=True)
            p = jnp.exp2(s - m)
            inv = 1.0 / jnp.sum(p, axis=0, keepdims=True)
            prob[e, :, rows] = p.astype(BF)
            inv_row[e * 8 + hh] = inv
            inv_rows = jnp.transpose(jnp.broadcast_to(inv, (HEAD, ROWS)))
            dos[e, rows, :] = (dos[e, rows, :].astype(F32) * inv_rows).astype(BF)
        acc[:, ecol] = nn(prob[e], dos[e])
        for i in range(KV_HEADS):
            at_head(e, i, lambda i=i: dv_start(i))
        return carry

    lax.fori_loop(0, KV_HEADS, first, 0)
    w_forward(3)
    l_recv()
    lab = lrcv[...].astype(F32)
    want = (c_i // BLK + 1).astype(F32)
    bwd_t[...] = jnp.where(same_row & (jnp.concatenate([lab, lab], axis=1) == want), 1.0, 0.0).astype(BF)
    w_forward(2)

    bsnd[...] = nn(bwd_t[...], dv_finish().astype(BF)).astype(BF)
    b_start()

    landed(tok.at[pl.ds(0, ROWS)], tl_sem.at[0])
    landed(tok.at[pl.ds(ROWS, ROWS)], tr_sem.at[0])

    def project(rows, blocks):
        total = None
        for dz, dy in blocks:
            zz, yy = up(z, dz), up(y, dy)
            cols = pl.ds(pl.multiple_of((zz * 4 + yy) * 256, 256), 256)
            term = nn(tok[rows, cols], wh[zz, yy])
            total = term if total is None else total + term
        return total

    near = [(dz, dy) for dz in (0, 1, 3) for dy in (0, 1, 3)]
    far = [(2, dy) for dy in range(4)] + [(dz, 2) for dz in (0, 1, 3)]
    part[...] = project(pl.ds(0, 512), near)
    w_end()


    give_part = remote(part.at[pl.ds(ROWS, ROWS)], part_in, p_s.at[0], p_r.at[0], sibling)
    part[pl.ds(ROWS, ROWS), :] += project(pl.ds(ROWS, ROWS), far)
    give_part.start()
    mine = part[pl.ds(0, ROWS), :] + project(pl.ds(0, ROWS), far)
    give_part.wait_recv()
    values = (mine + part_in[...]).astype(BF)
    snd[...] = nn(fwd[...], values).astype(BF)
    a_start()

    b_recv()
    dvl[pl.ds(0, ROWS), :] = tn(fwd[...], brcv[...]).astype(BF)
    give_dvl = remote(dvl.at[pl.ds(0, ROWS)], dvl.at[pl.ds(ROWS, ROWS)], d_s.at[0], d_r.at[0], sibling)
    give_dvl.start()
    give_dvl.wait_recv()

    def weight_blocks(i, carry):
        for n in range(8):
            cols = pl.ds(pl.multiple_of(i * 2048 + n * 256, 256), 256)
            wh[i * 2 + n // 4, n % 4] = tn(tok[:, cols], dvl[...]).astype(BF)
        return carry

    lax.fori_loop(0, 2, weight_blocks, 0)

    a_rows, b_rows = pl.ds(0, 128), pl.ds(128, 128)
    low2, high2 = pl.ds(0, 2), pl.ds(2, 2)

    g_1 = [
        remote(wh.at[up(z, 2), low2, a_rows], f1a, g_s.at[0], g_r.at[0], along_z(1)),
        remote(wh.at[up(z, 2), high2, a_rows], f2a, g_s.at[0], g_r.at[1], along_z(3)),
        remote(wh.at[low2, up(y, 2), b_rows], f1b, g_s.at[0], g_r.at[2], along_y(1)),
        remote(wh.at[high2, up(y, 2), b_rows], f2b, g_s.at[0], g_r.at[3], along_y(3)),
        remote(wh.at[up(z, 1), high2, a_rows], mpa.at[high2], g_s.at[0], g_r.at[4], along_z(1)),
        remote(wh.at[up(z, 3), low2, a_rows], mma.at[low2], g_s.at[0], g_r.at[5], along_z(3)),
        remote(wh.at[high2, up(y, 1), b_rows], mpb.at[high2], g_s.at[0], g_r.at[6], along_y(1)),
        remote(wh.at[low2, up(y, 3), b_rows], mmb.at[low2], g_s.at[0], g_r.at[7], along_y(3)),
    ]
    g_2 = [
        remote(wh.at[up(z, 1), low2, a_rows], mpa.at[low2], g_s.at[0], g_r.at[4], along_z(1)),
        remote(wh.at[up(z, 3), high2, a_rows], mma.at[high2], g_s.at[0], g_r.at[5], along_z(3)),
        remote(wh.at[low2, up(y, 1), b_rows], mpb.at[low2], g_s.at[0], g_r.at[6], along_y(1)),
        remote(wh.at[high2, up(y, 3), b_rows], mmb.at[high2], g_s.at[0], g_r.at[7], along_y(3)),
    ]

    def g_3a(o):
        return remote(wh.at[z, up(y, o), a_rows], s2a.at[o - 1], g2_s.at[0], g2_r.at[0], along_y(o))

    def g_3b(o):
        return remote(wh.at[up(z, o), y, b_rows], s2b.at[o - 1], g2_s.at[0], g2_r.at[1], along_z(o))

    def g_x(o):
        rows = pl.ds(up(x, o) * 64, 64)
        return remote(wh.at[z, y, rows], s3.at[o - 1], g3_s.at[0], g3_r.at[0], along_x(o))

    def bsum(*terms):
        total = terms[0].astype(F32)
        for t in terms[1:]:
            total = total + t.astype(F32)
        return total

    def g_step1():
        for i in range(4):
            g_1[i].wait_recv()
            if i == 0:
                wh[up(z, 1), 0:2, 0:128] = bsum(wh[up(z, 1), 0:2, 0:128], f1a[...]).astype(BF)
            elif i == 1:
                wh[up(z, 3), 2:4, 0:128] = bsum(wh[up(z, 3), 2:4, 0:128], f2a[...]).astype(BF)
            elif i == 2:
                wh[0:2, up(y, 1), 128:256] = bsum(wh[0:2, up(y, 1), 128:256], f1b[...]).astype(BF)
            else:
                wh[2:4, up(y, 3), 128:256] = bsum(wh[2:4, up(y, 3), 128:256], f2b[...]).astype(BF)
            g_2[i].start()

    def g_step2():
        for i, buf in enumerate((mpa, mma, mpb, mmb)):
            landed(buf, g_r.at[4 + i])
        for i in range(4):
            wh[z, i, 0:128] = bsum(wh[z, i, 0:128], mpa[i], mma[i]).astype(BF)
            wh[i, y, 128:256] = bsum(wh[i, y, 128:256], mpb[i], mmb[i]).astype(BF)
        for o in (1, 3, 2):
            g_3a(o).start()
            g_3b(o).start()

    def g_step3():
        landed(s2a, g2_r.at[0])
        landed(s2b, g2_r.at[1])
        wh[z, y, 0:128] = bsum(wh[z, y, 0:128], s2a[0], s2a[1], s2a[2]).astype(BF)
        wh[z, y, 128:256] = bsum(wh[z, y, 128:256], s2b[0], s2b[1], s2b[2]).astype(BF)
        for o in (1, 3, 2):
            g_x(o).start()

    def g_step4():
        landed(s3, g3_r.at[0])
        rows = pl.ds(pl.multiple_of(x * 64, 64), 64)
        wg_ref[...] = bsum(wh[z, y, rows, :], s3[0], s3[1], s3[2])
        landed(wh.at[pl.ds(0, 3)], g_s.at[0])
        landed(wh.at[0, pl.ds(0, 3)], g2_s.at[0])
        landed(s3, g3_s.at[0])

    for d in g_1[:4]:
        d.start()

    a_recv()
    mine_rows = pl.ds(pl.multiple_of(x * ROWS, ROWS), ROWS)
    vf[mine_rows, :] = tn(bwd_t[...], rcv[...]).astype(BF)

    def v_x(o, e):
        blk = vf.at[pl.ds(x * ROWS, ROWS), pl.ds(e * HEAD, HEAD)]
        return remote(blk, blk, v_s.at[0], v_r.at[e], along_x(o))

    def v_send(e):
        for o in (1, 3, 2):
            v_x(o, e).start()

    v_send(0)
    for d in g_1[4:]:
        d.start()
    v_send(1)
    for e in range(KV_HEADS):
        kt[e] = jnp.transpose(kf[:, pl.ds(e * HEAD, HEAD)].astype(F32)).astype(BF)

    def dq_out(h):
        return pltpu.make_async_copy(
            qs.at[h // 8, pl.ds((h % 8) * ROWS, ROWS)], dq_hbm.at[:, pl.ds(h * HEAD, HEAD)], dq_s.at[0])

    def second(e, carry):
        for i in range(KV_HEADS):
            @pl.when(e == i)
            def _():
                landed(three(i), v_r.at[i])
                if i < 2:
                    v_send(i + 2)
        at_head(e, 1, g_step1)
        at_head(e, 3, g_step2)
        ecol = pl.ds(pl.multiple_of(e * HEAD, HEAD), HEAD)
        values_e = vf[:, ecol]
        for hh in range(8):
            rows = slice(hh * ROWS, (hh + 1) * ROWS)
            dp = nt(values_e, dos[e, rows, :])
            p = prob[e, :, rows].astype(F32)
            rd = jnp.sum(p * dp, axis=0, keepdims=True) * inv_row[e * 8 + hh]
            prob[e, :, rows] = (p * (dp - rd)).astype(BF)
        acc[:, ecol] = nn(prob[e], qs[e])
        dq_t = nn(kt[e], prob[e]) * SCALE
        for hh in range(8):
            rows = slice(hh * ROWS, (hh + 1) * ROWS)
            qs[e, rows, :] = jnp.transpose(dq_t[:, rows]).astype(BF)
        for hh in range(8):
            dq_out(e * 8 + hh).start()
        for i in range(KV_HEADS):
            at_head(e, i, lambda i=i: dk_start(i))
        return carry

    lax.fori_loop(0, KV_HEADS, second, 0)

    g_step3()
    dk_ref[...] = (dk_finish() * SCALE).astype(BF)
    g_step4()

    landed(qs, dq_s.at[0])
    landed(kf.at[pl.ds(0, 768)], k_s.at[0])
    landed(vf.at[pl.ds(0, 768)], v_s.at[0])
    l_done()
    a_done()
    b_done()
    give_part.wait_send()
    give_dvl.wait_send()

    landed(tok.at[pl.ds(ROWS, ROWS)], ts_sem.at[0])


def hand_on(dq_in, dk_in, wg_in, dq_out, dk_out, wg_out, dq_v, dk_v, wg_v, sem):
    steps = [(dk_in, dk_v, dk_out), (wg_in, wg_v, wg_out)]
    for i in range(8):
        rows = pl.ds(i * 32, 32)
        steps.append((dq_in.at[rows], dq_v.at[rows], dq_out.at[rows]))
    into = [pltpu.make_async_copy(a, v, sem.at[0, i]) for i, (a, v, _) in enumerate(steps)]
    away = [pltpu.make_async_copy(v, b, sem.at[1, i]) for i, (_, v, b) in enumerate(steps)]
    for copy in into:
        copy.start()
    for i, copy in enumerate(into):
        copy.wait()
        away[i].start()
    for copy in away:
        copy.wait()


def per_device(tokens, w, queries, keys, cotangent, block_dest, doc_ids):
    vm = lambda shape, t: pltpu.VMEM(shape, t)
    dma = lambda n: pltpu.SemaphoreType.DMA((n,))
    anyspec = pl.BlockSpec(memory_space=pl.ANY)
    vspec = pl.BlockSpec(memory_space=pltpu.VMEM)
    scratch = [
        vm((512, 4096), BF),
        vm((4, 4, 256, FEAT), BF),
        vm((KV_HEADS, 8 * ROWS, HEAD), BF),
        vm((KV_HEADS, 8 * ROWS, HEAD), BF),
        vm((KEYS, FEAT), BF),
        vm((KV_HEADS, HEAD, KEYS), BF),
        vm((KEYS, FEAT), BF),
        vm((KV_HEADS, KEYS, 8 * ROWS), BF),
        vm((HEADS, 1, ROWS), F32),
        vm((KEYS, ROWS), F32),
        vm((KEYS, FEAT), F32),
        vm((2 * ROWS, FEAT), F32),
        vm((ROWS, FEAT), F32),
        vm((SLOTS, FEAT), BF),
        vm((SLOTS, FEAT), BF),
        vm((SLOTS, 128), BF),
        vm((SLOTS, 128), BF),
        vm((SLOTS, ROWS), BF),
        vm((SLOTS, ROWS), BF),
        vm((SLOTS, FEAT), BF),
        vm((SLOTS, FEAT), BF),
        vm((512, FEAT), BF),
        vm((KEYS, FEAT), BF),
        vm((3, ROWS, FEAT), BF),
        vm((2, 128, FEAT), BF),
        vm((2, 128, FEAT), BF),
        vm((2, 128, FEAT), BF),
        vm((2, 128, FEAT), BF),
        vm((4, 128, FEAT), BF),
        vm((4, 128, FEAT), BF),
        vm((4, 128, FEAT), BF),
        vm((4, 128, FEAT), BF),
        vm((3, 128, FEAT), BF),
        vm((3, 128, FEAT), BF),
        vm((3, 64, FEAT), BF),
        dma(2), dma(4), dma(4), dma(1), dma(1), dma(1),
        dma(1), dma(1), dma(1), dma(8), dma(1), dma(17), dma(1), dma(4),
        dma(1), dma(1), dma(1), dma(1), dma(1), dma(1),
        dma(1), dma(1), dma(1), dma(1),
        dma(1), dma(4), dma(1), dma(1), dma(1), dma(1),
        dma(1), dma(8), dma(1), dma(2), dma(1), dma(1), dma(1),
        pltpu.SemaphoreType.REGULAR,
    ]
    raw = pl.pallas_call(
        kernel,
        out_shape=(
            jax.ShapeDtypeStruct((ROWS, 4096), BF),
            jax.ShapeDtypeStruct((ROWS, FEAT), BF),
            jax.ShapeDtypeStruct((64, FEAT), F32),
        ),
        in_specs=[anyspec] * 5 + [pl.BlockSpec(memory_space=pltpu.SMEM), vspec],
        out_specs=(anyspec, vspec, vspec),
        scratch_shapes=scratch,
        compiler_params=pltpu.CompilerParams(
            collective_id=0, has_side_effects=True, vmem_limit_bytes=62 * 1024 * 1024
        ),
        name="attention_and_weights",
    )(tokens, w, queries, keys, cotangent, block_dest, doc_ids)
    return pl.pallas_call(
        hand_on,
        out_shape=tuple(jax.ShapeDtypeStruct(r.shape, r.dtype) for r in raw),
        in_specs=[anyspec] * 3,
        out_specs=(anyspec,) * 3,
        scratch_shapes=[
            vm((ROWS, 4096), BF), vm((ROWS, FEAT), BF), vm((64, FEAT), F32), pltpu.SemaphoreType.DMA((2, 10))],
        name="hand_on",
    )(*raw)


def solution(mesh):
    both = P(("dp", "sp"), None)
    return jax.shard_map(
        per_device,
        mesh=mesh,
        in_specs=(both, both, both, both, both, P(("dp", "sp")), P("dp", None)),
        out_specs=(both, both, both),
        check_vma=False,
    )
```
